256 devices in a mesh: row: 16 (over z, x_lo), col: 16 (over y, x_hi, core).
Axes of the slice: x: 4 (x_hi: 2, x_lo: 2; x = x_hi * 2 + x_lo), y: 4, z: 8, core: 2. Of those that a mesh axis runs over, the one named last changes fastest.
Arguments:
- a_matrix: bfloat16 [12288, 12288], P('row', 'col'), may hold values from -0.1875 to 0.1875
- prolong: bfloat16 [12288, 2048], P('row', 'col'), may hold values from -1 to 1
- a_pattern: int32 [96, 96], P('row', 'col'), may hold values from 0 to 1, as said below
- p_pattern: int32 [96, 16], P('row', 'col'), may hold values from 0 to 1, as said below
Outputs:
- coarse: float32 [2048, 2048], P('row', 'col')
The draws below stay inside these ranges and needn't reach their ends.
Inputs may be any that keep to these rules, and one draw needn't show every extreme that they name: `a_pattern`: symmetric; every diagonal block is stored. `p_pattern`: every fine block row stores at least one coarse block.
All inputs are finite; a program needn't handle non-finite values.
Results may differ from the reference program's by a relative error of at most 0.0029.
Values may be sent and summed in bfloat16 or wider, within the bound.
No kernel may reach another device: no remote copies, remote signals or barrier semaphores. Data moves between devices by JAX's collectives and lax.ppermute only.
A program may use at most 128 MiB of HBM per device.

```python
import jax
import jax.numpy as jnp

BLOCK = 128
NFB = 96
NCB = 16
NF = 12288
NC = 2048


def draw_a_pattern(key, part):
    key = jax.random.fold_in(key, 11)
    index = jnp.arange(NFB, dtype=jnp.int32)
    coins = jax.random.randint(key, (NFB, NFB), 0, 5, dtype=jnp.int32)
    chosen = coins == 0
    diagonal = index[:, None] == index[None, :]
    joined = chosen | chosen.T | diagonal
    return joined.astype(jnp.int32)


def draw_p_pattern(key, part):
    key = jax.random.fold_in(key, 23)
    first_key = jax.random.fold_in(key, 1)
    second_key = jax.random.fold_in(key, 2)
    columns = jnp.arange(NCB, dtype=jnp.int32)
    anchor = jax.random.randint(first_key, (NFB,), 0, NCB, dtype=jnp.int32)
    coins = jax.random.randint(second_key, (NFB, NCB), 0, 10, dtype=jnp.int32)
    own = columns[None, :] == anchor[:, None]
    extra = coins < 3
    return (own | extra).astype(jnp.int32)


def shard_levels(rng, extent, split, least, high):
    def one(position, parts):
        steps = jax.random.uniform(jax.random.fold_in(jax.random.fold_in(rng, 6), position), (parts,), jnp.float32, least / len(split), high / len(split))
        return jnp.repeat(jnp.exp(steps), extent[position] // parts).reshape((-1,) + (1,) * (len(extent) - position - 1))

    loudness = one(*split[0])
    for cut in split[1:]:
        loudness = loudness * one(*cut)
    return loudness


def normal_values(stream_key, extent, spread, reach, cuts=(), kind=jnp.bfloat16):
    result = spread * jax.random.normal(stream_key, extent, jnp.float32)
    if cuts:
        result = result * shard_levels(stream_key, extent, cuts, -0.22, 0.18)
    return jnp.clip(result, -reach, reach).astype(kind)


def setup_inputs(seed: int = 0) -> dict:
    arg_keys = jax.random.split(jax.random.key(seed), 5)
    a_matrix = normal_values(arg_keys[0], (NF, NF), (9 * BLOCK) ** -0.5, 0.1875, ((0, 16), (1, 16)))
    prolong = normal_values(arg_keys[1], (NF, NC), (BLOCK // 4) ** -0.5, 1.0, ((0, 16), (1, 16)))
    a_pattern = draw_a_pattern(jax.random.fold_in(arg_keys[4], 71), 0)
    p_pattern = draw_p_pattern(jax.random.fold_in(arg_keys[4], 71), 0)
    return {"a_matrix": a_matrix, "prolong": prolong, "a_pattern": a_pattern, "p_pattern": p_pattern}


def expand(pattern, width):
    return jnp.repeat(jnp.repeat(pattern, width, axis=0), width, axis=1).astype(jnp.bfloat16)


def reference(a_matrix, prolong, a_pattern, p_pattern):
    a_eff = a_matrix * expand(a_pattern, BLOCK)
    p_eff = prolong * expand(p_pattern, BLOCK)
    w_full = jnp.dot(a_eff, p_eff, preferred_element_type=jnp.float32).astype(jnp.bfloat16)
    return jnp.dot(p_eff.T, w_full, preferred_element_type=jnp.float32)
```

```python
import jax
import jax.numpy as jnp
from jax import lax
from jax.sharding import PartitionSpec as P

BLOCK = 128
AXES = ("row", "col")
PLANES, LANES = 8, 4


def place(z, xl, y, xh, k):
    return (2 * (z % PLANES) + xl) * 16 + 4 * (y % LANES) + 2 * xh + k


SPOTS = [
    (z, xl, y, xh, k)
    for z in range(PLANES)
    for xl in range(2)
    for y in range(LANES)
    for xh in range(2)
    for k in range(2)
]


def send(value, target):
    pairs = [(place(*spot), place(*target(*spot))) for spot in SPOTS]
    return lax.ppermute(value, AXES, pairs)


def turn(z, xl, y, xh, k):
    shift = (y - z // 2) % LANES
    return (z + shift if z % 2 else z - shift), xl, z // 2, xh, k


def z_up(z, xl, y, xh, k):
    return z + 1, xl, y, xh, k


def z_down(z, xl, y, xh, k):
    return z - 1, xl, y, xh, k


def y_up(z, xl, y, xh, k):
    return z, xl, y + 1, xh, k


def y_down(z, xl, y, xh, k):
    return z, xl, y - 1, xh, k


def far_x(z, xl, y, xh, k):
    return z, xl, y, 1 - xh, k


def other_core(z, xl, y, xh, k):
    return z, xl, y, xh, 1 - k


def swap(z, xl, y, xh, k):
    return z, k, y, xh, xl


def swap_far(z, xl, y, xh, k):
    return z, k, y, 1 - xh, xl


W_GROUPS = [
    [place(z, s ^ k, y, xh, k) for s in range(2) for y in range(LANES)]
    for z in range(PLANES)
    for xh in range(2)
    for k in range(2)
]


def coarse_row(y, xh, k, dk, dy, dx):
    i = 4 * ((y - dy) % LANES) + 2 * (xh ^ dx) + (k ^ dk)
    return i // 2, i % 2


C_GROUPS = [
    [
        place(*coarse_row(y, xh, k, dk, dy, dx), y, xh, k)
        for dk in range(2)
        for dy in range(LANES)
        for dx in range(2)
    ]
    for y in range(LANES)
    for xh in range(2)
    for k in range(2)
]


def expand(pattern, width):
    return jnp.repeat(jnp.repeat(pattern, width, axis=0), width, axis=1).astype(jnp.bfloat16)


def dot32(a, b, contract=((1,), (0,))):
    return lax.dot_general(a, b, (contract, ((), ())), preferred_element_type=jnp.float32)


def column_rows(pair):
    pairs = [pair]
    for _ in range(LANES - 1):
        pairs.append(send(pairs[-1], y_up))
    own = jnp.concatenate(pairs)
    return jnp.concatenate([own, send(own, other_core)])


def pack(c_part):
    top = jnp.maximum(jnp.max(jnp.abs(c_part)), 1e-30)
    power = jnp.ceil(jnp.log2(top)) - 14.0
    scaled = c_part * jnp.exp2(-power)
    tail = jnp.full((c_part.shape[0], 16, c_part.shape[2]), power)
    return jnp.concatenate([scaled, tail], axis=1).astype(jnp.float16)


def unpack(parts):
    parts = parts.astype(jnp.float32)
    return jnp.sum(parts[:, :BLOCK] * jnp.exp2(parts[:, BLOCK : BLOCK + 1, :1]), axis=0)


def fine_rows(first):
    half = first.shape[0] // 2
    up, down = [first], [first]
    for step in range(1, 4):
        both = lax.optimization_barrier((send(up[-1], z_up), send(down[-1], z_down)))
        up.append(both[0])
        down.append(both[1])
    far = jnp.concatenate([send(up[3][:half], z_up), send(down[3][half:], z_down)])
    return jnp.stack([first, down[1], down[2], down[3], far, up[3], up[2], up[1]])


def local(a_matrix, prolong, a_pattern, p_pattern):
    row, col = lax.axis_index("row"), lax.axis_index("col")
    z, y, xh = row // 2, col // 4, (col // 2) % 2
    p_eff = prolong * expand(p_pattern, BLOCK)
    p_eff, a_matrix = lax.optimization_barrier((p_eff, a_matrix))
    first = send(p_eff, turn)
    a_eff = a_matrix * expand(a_pattern, BLOCK)
    near, distant = send(a_eff, swap), send(a_eff, swap_far)
    pair = jnp.stack([p_eff, send(p_eff, far_x)])
    first, pair, _ = lax.optimization_barrier((first, pair, a_eff))
    blocks = fine_rows(first)
    near_2, distant_2 = send(near, other_core), send(distant, other_core)
    p_wide = column_rows(pair)

    def columns(flip):
        odd = flip ^ xh
        shifts = [lax.rem(yy - y + LANES, LANES) for yy in range(LANES)]
        picks = [2 * y + jnp.where(odd == 1, 1 + s, -s) - z for s in shifts]
        return jnp.stack(
            [lax.dynamic_index_in_dim(blocks, (i + 2 * PLANES) % PLANES, keepdims=False) for i in picks]
        )

    p_0, p_1 = columns(0), columns(1)

    def product(a, p):
        return jnp.einsum("rc,ycj->yrj", a, p, preferred_element_type=jnp.float32)

    w_part = jnp.concatenate(
        [
            (product(near, p_0) + product(distant, p_1)).astype(jnp.bfloat16),
            (product(near_2, p_0) + product(distant_2, p_1)).astype(jnp.bfloat16),
        ]
    )
    w_parts = lax.all_to_all(w_part, AXES, 0, 0, axis_index_groups=W_GROUPS, tiled=True)
    w = jnp.sum(w_parts.astype(jnp.float32), axis=0)
    w_high = lax.reduce_precision(w, 8, 7)
    w_both = jnp.concatenate([w_high, w - w_high], axis=1).astype(jnp.bfloat16)
    c_both = dot32(p_wide, w_both)
    c_part = c_both[..., :BLOCK] + c_both[..., BLOCK:]
    return unpack(lax.all_to_all(pack(c_part), AXES, 0, 0, axis_index_groups=C_GROUPS, tiled=True))


def solution(mesh):
    placed = (P("row", "col"),) * 4
    return jax.shard_map(
        local, mesh=mesh, in_specs=placed, out_specs=P("row", "col"), check_vma=False
    )
```

```python
import functools

import jax
import jax.numpy as jnp
from jax import lax
from jax.experimental import pallas as pl
from jax.experimental.pallas import tpu as pltpu
from jax.sharding import PartitionSpec as P

BLOCK = 128
AXES = ("row", "col")
PLANES, LANES = 8, 4


def place(z, xl, y, xh, k):
    return (2 * (z % PLANES) + xl) * 16 + 4 * (y % LANES) + 2 * xh + k


SPOTS = [
    (z, xl, y, xh, k)
    for z in range(PLANES)
    for xl in range(2)
    for y in range(LANES)
    for xh in range(2)
    for k in range(2)
]


def send(value, target):
    pairs = [(place(*spot), place(*target(*spot))) for spot in SPOTS]
    return lax.ppermute(value, AXES, pairs)


def turn(z, xl, y, xh, k):
    shift = (y - z // 2) % LANES
    return (z + shift if z % 2 else z - shift), xl, z // 2, xh, k


def z_up(z, xl, y, xh, k):
    return z + 1, xl, y, xh, k


def z_down(z, xl, y, xh, k):
    return z - 1, xl, y, xh, k


def y_up(z, xl, y, xh, k):
    return z, xl, y + 1, xh, k


def y_down(z, xl, y, xh, k):
    return z, xl, y - 1, xh, k


def far_x(z, xl, y, xh, k):
    return z, xl, y, 1 - xh, k


def other_core(z, xl, y, xh, k):
    return z, xl, y, xh, 1 - k


def swap(z, xl, y, xh, k):
    return z, k, y, xh, xl


def swap_far(z, xl, y, xh, k):
    return z, k, y, 1 - xh, xl


W_GROUPS = [
    [place(z, s ^ k, y, xh, k) for s in range(2) for y in range(LANES)]
    for z in range(PLANES)
    for xh in range(2)
    for k in range(2)
]


def coarse_row(y, xh, k, dk, dy, dx):
    i = 4 * ((y - dy) % LANES) + 2 * (xh ^ dx) + (k ^ dk)
    return i // 2, i % 2


C_GROUPS = [
    [
        place(*coarse_row(y, xh, k, dk, dy, dx), y, xh, k)
        for dk in range(2)
        for dy in range(LANES)
        for dx in range(2)
    ]
    for y in range(LANES)
    for xh in range(2)
    for k in range(2)
]


VMEM = pl.BlockSpec(memory_space=pltpu.VMEM)
SMEM = pl.BlockSpec(memory_space=pltpu.SMEM)


def on_device(kernel, shape, dtype, specs, scratch=(), cost=None, grant=1):
    return pl.pallas_call(
        kernel,
        out_shape=jax.ShapeDtypeStruct(shape, dtype),
        in_specs=specs,
        out_specs=VMEM,
        scratch_shapes=scratch,
        compiler_params=pltpu.CompilerParams(vmem_limit_bytes=grant << 20),
        cost_estimate=cost,
    )


def dot32(a, b):
    return jnp.dot(a, b, preferred_element_type=jnp.float32)


def masked(value, pattern):
    wide = jnp.repeat(jnp.repeat(pattern, BLOCK, axis=0), BLOCK, axis=1)
    return value * wide.astype(value.dtype)


def mask_kernel(pattern_ref, value_ref, out_ref):
    for i in range(pattern_ref.shape[0]):
        for j in range(pattern_ref.shape[1]):
            spot = (slice(i * BLOCK, (i + 1) * BLOCK), slice(j * BLOCK, (j + 1) * BLOCK))
            value = value_ref[spot]
            out_ref[spot] = jnp.where(pattern_ref[i, j] != 0, value, jnp.zeros_like(value))


def masked_tile(value, pattern):
    cost = pl.CostEstimate(flops=value.size, bytes_accessed=4 * value.size, transcendentals=0)
    return on_device(mask_kernel, value.shape, value.dtype, [SMEM, VMEM], cost=cost)(pattern, value)


def pair_kernel(one, two, out_ref):
    out_ref[0] = one[...]
    out_ref[1] = two[...]


def paired(one, two):
    cost = pl.CostEstimate(flops=0, bytes_accessed=8 * one.size, transcendentals=0)
    return on_device(pair_kernel, (2, *one.shape), one.dtype, [VMEM] * 2, cost=cost)(one, two)


def line_up_kernel(spot_ref, *refs):
    blocks, p_ref = refs[:9], refs[9]
    z, y, xh = spot_ref[0], spot_ref[1], spot_ref[2]
    half = blocks[4].shape[0]
    for d in range(PLANES):
        place_in = lax.rem(z + d - 2 * y - 1 + 2 * PLANES, PLANES)
        odd = (place_in < LANES).astype(jnp.int32)
        shift = jnp.where(odd == 1, place_in, PLANES - 1 - place_in)
        side = lax.rem(odd + xh, 2)
        column = pl.multiple_of(lax.rem(y + shift, LANES) * BLOCK, BLOCK)
        if d < 4:
            p_ref[side, :, pl.ds(column, BLOCK)] = blocks[d][...]
        elif d == 4:
            p_ref[side, :half, pl.ds(column, BLOCK)] = blocks[4][...]
            p_ref[side, half:, pl.ds(column, BLOCK)] = blocks[5][...]
        else:
            p_ref[side, :, pl.ds(column, BLOCK)] = blocks[d + 1][...]


def line_up(spot, blocks):
    size = blocks[0].shape[0]
    return on_device(
        line_up_kernel, (2, size, LANES * BLOCK), jnp.bfloat16, [SMEM] + [VMEM] * len(blocks),
        cost=pl.CostEstimate(flops=0, bytes_accessed=4 << 20, transcendentals=0),
    )(spot, *blocks)


def w_kernel(base, p_ref, one, two, *rest):
    out_ref = rest[-1]
    if base:
        out_ref[:base] = rest[0][...]
    size = one.shape[0]
    step = size // 3
    for c in range(0, LANES, 2):
        columns = slice(c * BLOCK, (c + 2) * BLOCK)
        for start in range(0, size, step):
            rows = slice(start, start + step)
            total = dot32(one[rows], p_ref[0, :, columns]) + dot32(two[rows], p_ref[1, :, columns])
            total = total.astype(jnp.bfloat16)
            out_ref[base + c, rows] = total[:, :BLOCK]
            out_ref[base + c + 1, rows] = total[:, BLOCK:]


def w_products(p_all, one, two, *before):
    size = one.shape[0]
    return on_device(
        functools.partial(w_kernel, LANES * len(before)),
        (LANES * (1 + len(before)), size, BLOCK),
        jnp.bfloat16,
        [VMEM] * (3 + len(before)),
        cost=pl.CostEstimate(flops=4 * size * size * LANES * BLOCK, bytes_accessed=6 << 20, transcendentals=0),
        grant=6,
    )(p_all, one, two, *before)


def c_kernel(parts_ref, *refs):
    pairs, (out_ref, w_ref) = refs[: 2 * LANES], refs[2 * LANES :]
    w = parts_ref[0].astype(jnp.float32)
    for i in range(1, parts_ref.shape[0]):
        w += parts_ref[i].astype(jnp.float32)
    turned = w.T
    high = turned.astype(jnp.bfloat16)
    w_ref[:BLOCK] = high
    w_ref[BLOCK:] = (turned - high.astype(jnp.float32)).astype(jnp.bfloat16)
    units = [pair.at[i] for pair in pairs for i in range(2)]
    top = jnp.zeros((BLOCK, BLOCK), jnp.float32)
    for i, unit in enumerate(units):
        both = dot32(w_ref[...], unit[...])
        part = both[:BLOCK] + both[BLOCK:]
        out_ref[i, :BLOCK] = part
        top = jnp.maximum(top, jnp.abs(part))
    top = jnp.max(jnp.max(top, axis=0, keepdims=True), axis=1, keepdims=True)
    power = jnp.ceil(jnp.log2(jnp.maximum(top, 1e-30))) - 14.0
    scale = jnp.exp2(-power)
    for i in range(len(units)):
        out_ref[i, :BLOCK] = out_ref[i, :BLOCK] * scale
        out_ref[i, BLOCK:] = jnp.broadcast_to(power, (8, BLOCK))


def c_products(parts, pairs):
    size = parts.shape[1]
    return on_device(
        c_kernel,
        (4 * LANES, BLOCK + 8, BLOCK),
        jnp.float32,
        [VMEM] * (2 * LANES + 1),
        [pltpu.VMEM((2 * BLOCK, size), jnp.bfloat16)],
        pl.CostEstimate(flops=16 * LANES * size * BLOCK * BLOCK, bytes_accessed=6 << 20, transcendentals=0),
        grant=8,
    )(parts, *pairs)


def unpack(parts):
    parts = parts.astype(jnp.float32)
    return jnp.sum(parts[:, :BLOCK] * jnp.exp2(parts[:, BLOCK : BLOCK + 1, :1]), axis=0).T


def both(*values):
    return lax.optimization_barrier(values)


def local(a_matrix, prolong, a_pattern, p_pattern):
    row, col = lax.axis_index("row"), lax.axis_index("col")
    spot = jnp.stack([row // 2, col // 4, (col // 2) % 2]).astype(jnp.int32)
    p_eff = masked(prolong, p_pattern)
    p_eff, a_matrix = both(p_eff, a_matrix)
    first, across = send(p_eff, turn), send(p_eff, far_x)
    a_eff = masked_tile(a_matrix, a_pattern)
    near, distant = send(a_eff, swap), send(a_eff, swap_far)
    first, p_eff, across, spot, _ = both(first, p_eff, across, spot, a_eff)
    pair = paired(p_eff, across)
    up_1, down_1 = both(send(first, z_up), send(first, z_down))
    below = send(pair, y_up)
    up_2, down_2 = both(send(up_1, z_up), send(down_1, z_down))
    up_2, down_2, below = both(up_2, down_2, below)
    beyond = send(below, y_up)
    up_3, down_3 = both(send(up_2, z_up), send(down_2, z_down))
    up_3, down_3, beyond = both(up_3, down_3, beyond)
    half = first.shape[0] // 2
    far = [send(up_3[:half], z_up), send(down_3[half:], z_down)]
    above = send(beyond, y_up)
    *far, near, distant, above = both(*far, near, distant, above)
    p_all = line_up(spot, [first, down_1, down_2, down_3, *far, up_3, up_2, up_1])
    near_2, distant_2 = send(near, other_core), send(distant, other_core)
    w_part = w_products(p_all, near, distant)
    w_part = w_products(p_all, near_2, distant_2, w_part)
    w_part, *pairs = both(w_part, pair, below, beyond, above)
    pairs += [send(p, other_core) for p in pairs]
    w_parts = lax.all_to_all(w_part, AXES, 0, 0, axis_index_groups=W_GROUPS, tiled=True)
    c_part = c_products(w_parts, pairs).astype(jnp.float16)
    return unpack(lax.all_to_all(c_part, AXES, 0, 0, axis_index_groups=C_GROUPS, tiled=True))


def solution(mesh):
    placed = (P("row", "col"),) * 4
    return jax.shard_map(
        local, mesh=mesh, in_specs=placed, out_specs=P("row", "col"), check_vma=False
    )
```

```python
import functools

import jax
import jax.numpy as jnp
from jax import lax
from jax.experimental import pallas as pl
from jax.experimental.pallas import tpu as pltpu
from jax.sharding import PartitionSpec as P

BLOCK = 128
AXES = ("row", "col")
PLANES, LANES = 8, 4


def place(z, xl, y, xh, k):
    return (2 * (z % PLANES) + xl) * 16 + 4 * (y % LANES) + 2 * xh + k


SPOTS = [
    (z, xl, y, xh, k)
    for z in range(PLANES)
    for xl in range(2)
    for y in range(LANES)
    for xh in range(2)
    for k in range(2)
]


def send(value, target):
    pairs = [(place(*spot), place(*target(*spot))) for spot in SPOTS]
    return lax.ppermute(value, AXES, pairs)


def turn(z, xl, y, xh, k):
    shift = (y - z // 2) % LANES
    return (z + shift if z % 2 else z - shift), xl, z // 2, xh, k


def turn_far(z, xl, y, xh, k):
    z_to, *rest = turn(z, xl, y, xh, k)
    return z_to + PLANES // 2, *rest


def z_up(z, xl, y, xh, k):
    return z + 1, xl, y, xh, k


def z_down(z, xl, y, xh, k):
    return z - 1, xl, y, xh, k


def y_up(z, xl, y, xh, k):
    return z, xl, y + 1, xh, k


def y_down(z, xl, y, xh, k):
    return z, xl, y - 1, xh, k


def far_x(z, xl, y, xh, k):
    return z, xl, y, 1 - xh, k


def other_core(z, xl, y, xh, k):
    return z, xl, y, xh, 1 - k


def swap(z, xl, y, xh, k):
    return z, k, y, xh, xl


def swap_far(z, xl, y, xh, k):
    return z, k, y, 1 - xh, xl


W_GROUPS = [
    [place(z, s ^ k, y, xh, k) for s in range(2) for y in range(LANES)]
    for z in range(PLANES)
    for xh in range(2)
    for k in range(2)
]


def coarse_row(y, xh, k, dk, dy, dx):
    i = 4 * ((y - dy) % LANES) + 2 * (xh ^ dx) + (k ^ dk)
    return i // 2, i % 2


C_GROUPS = [
    [
        place(*coarse_row(y, xh, k, dk, dy, dx), y, xh, k)
        for dk in range(2)
        for dy in range(LANES)
        for dx in range(2)
    ]
    for y in range(LANES)
    for xh in range(2)
    for k in range(2)
]


VMEM = pl.BlockSpec(memory_space=pltpu.VMEM)
SMEM = pl.BlockSpec(memory_space=pltpu.SMEM)


def on_device(kernel, shape, dtype, specs, scratch=(), cost=None, grant=1):
    return pl.pallas_call(
        kernel,
        out_shape=jax.ShapeDtypeStruct(shape, dtype),
        in_specs=specs,
        out_specs=VMEM,
        scratch_shapes=scratch,
        compiler_params=pltpu.CompilerParams(vmem_limit_bytes=grant << 20),
        cost_estimate=cost,
    )


def dot32(a, b):
    return jnp.dot(a, b, preferred_element_type=jnp.float32)


def masked(value, pattern):
    wide = jnp.repeat(jnp.repeat(pattern, BLOCK, axis=0), BLOCK, axis=1)
    return value * wide.astype(value.dtype)


def mask_kernel(token_ref, pattern_ref, value_ref, out_ref):
    for i in range(pattern_ref.shape[0]):
        for j in range(pattern_ref.shape[1]):
            spot = (slice(i * BLOCK, (i + 1) * BLOCK), slice(j * BLOCK, (j + 1) * BLOCK))
            value = value_ref[spot]
            out_ref[spot] = jnp.where(pattern_ref[i, j] != 0, value, jnp.zeros_like(value))


def masked_tile(token, value, pattern):
    cost = pl.CostEstimate(flops=value.size, bytes_accessed=4 * value.size, transcendentals=0)
    return on_device(mask_kernel, value.shape, value.dtype, [SMEM, SMEM, VMEM], cost=cost)(token, pattern, value)


def pair_kernel(one, two, out_ref):
    out_ref[0] = one[...]
    out_ref[1] = two[...]


def paired(one, two):
    cost = pl.CostEstimate(flops=0, bytes_accessed=8 * one.size, transcendentals=0)
    return on_device(pair_kernel, (2, *one.shape), one.dtype, [VMEM] * 2, cost=cost)(one, two)


def line_up_kernel(spot_ref, own, above, below, up_two, down_two, p_ref):
    z, y, xh = spot_ref[0], spot_ref[1], spot_ref[2]
    blocks = [own.at[0], above.at[0], down_two, below.at[1], own.at[1], above.at[1], up_two, below.at[0]]
    for d, block in enumerate(blocks):
        place_in = lax.rem(z + d - 2 * y - 1 + 2 * PLANES, PLANES)
        odd = (place_in < LANES).astype(jnp.int32)
        shift = jnp.where(odd == 1, place_in, PLANES - 1 - place_in)
        side = lax.rem(odd + xh, 2)
        column = pl.multiple_of(lax.rem(y + shift, LANES) * BLOCK, BLOCK)
        p_ref[side, :, pl.ds(column, BLOCK)] = block[...]


def line_up(spot, *blocks):
    size = blocks[0].shape[1]
    return on_device(
        line_up_kernel, (2, size, LANES * BLOCK), jnp.bfloat16, [SMEM] + [VMEM] * len(blocks),
        cost=pl.CostEstimate(flops=0, bytes_accessed=4 << 20, transcendentals=0),
    )(spot, *blocks)


def w_kernel(base, p_ref, one, two, *rest):
    out_ref = rest[-1]
    if base:
        out_ref[:base] = rest[0][...]
    size = one.shape[0]
    step = size // 3
    for c in range(0, LANES, 2):
        columns = slice(c * BLOCK, (c + 2) * BLOCK)
        for start in range(0, size, step):
            rows = slice(start, start + step)
            total = dot32(one[rows], p_ref[0, :, columns]) + dot32(two[rows], p_ref[1, :, columns])
            total = total.astype(jnp.bfloat16)
            out_ref[base + c, rows] = total[:, :BLOCK]
            out_ref[base + c + 1, rows] = total[:, BLOCK:]


def w_products(p_all, one, two, *before):
    size = one.shape[0]
    return on_device(
        functools.partial(w_kernel, LANES * len(before)),
        (LANES * (1 + len(before)), size, BLOCK),
        jnp.bfloat16,
        [VMEM] * (3 + len(before)),
        cost=pl.CostEstimate(flops=4 * size * size * LANES * BLOCK, bytes_accessed=6 << 20, transcendentals=0),
        grant=3,
    )(p_all, one, two, *before)


def c_kernel(parts_ref, *refs):
    pairs, (out_ref, w_ref) = refs[: 2 * LANES], refs[2 * LANES :]
    for start in range(0, parts_ref.shape[1], BLOCK):
        rows = slice(start, start + BLOCK)
        w = parts_ref[0, rows].astype(jnp.float32)
        for i in range(1, parts_ref.shape[0]):
            w += parts_ref[i, rows].astype(jnp.float32)
        turned = w.T
        high = turned.astype(jnp.bfloat16)
        w_ref[:BLOCK, rows] = high
        w_ref[BLOCK:, rows] = (turned - high.astype(jnp.float32)).astype(jnp.bfloat16)
    units = [pair.at[i] for pair in pairs for i in range(2)]
    top = jnp.zeros((BLOCK, BLOCK), jnp.float32)
    for i, unit in enumerate(units):
        both = dot32(w_ref[...], unit[...])
        part = both[:BLOCK] + both[BLOCK:]
        out_ref[i, :BLOCK] = part
        top = jnp.maximum(top, jnp.abs(part))
    top = jnp.max(jnp.max(top, axis=0, keepdims=True), axis=1, keepdims=True)
    power = jnp.ceil(jnp.log2(jnp.maximum(top, 1e-30))) - 14.0
    scale = jnp.exp2(-power)
    for i in range(len(units)):
        out_ref[i, :BLOCK] = out_ref[i, :BLOCK] * scale
        out_ref[i, BLOCK:] = jnp.broadcast_to(power, (8, BLOCK))


def c_products(parts, pairs):
    size = parts.shape[1]
    return on_device(
        c_kernel,
        (4 * LANES, BLOCK + 8, BLOCK),
        jnp.float32,
        [VMEM] * (2 * LANES + 1),
        [pltpu.VMEM((2 * BLOCK, size), jnp.bfloat16)],
        pl.CostEstimate(flops=16 * LANES * size * BLOCK * BLOCK, bytes_accessed=6 << 20, transcendentals=0),
        grant=2,
    )(parts, *pairs)


def unpack(parts):
    parts = parts.astype(jnp.float32)
    return jnp.sum(parts[:, :BLOCK] * jnp.exp2(parts[:, BLOCK : BLOCK + 1, :1]), axis=0).T


def both(*values):
    return lax.optimization_barrier(values)


def local(a_matrix, prolong, a_pattern, p_pattern):
    row, col = lax.axis_index("row"), lax.axis_index("col")
    spot = jnp.stack([row // 2, col // 4, (col // 2) % 2]).astype(jnp.int32)
    p_eff = masked(prolong, p_pattern)
    p_eff, spot = both(p_eff, spot)
    first, second = send(p_eff, turn), send(p_eff, turn_far)
    across = send(p_eff, far_x)
    a_eff = masked_tile(spot, a_matrix, a_pattern)
    a_eff, across = both(a_eff, across)
    near, distant = send(a_eff, swap), send(a_eff, swap_far)
    pair = paired(p_eff, across)
    first, second, _ = both(first, second, a_eff)
    own = paired(first, second)
    below, above, pair_1 = both(send(own, z_up), send(own, z_down), send(pair, y_up))
    pair_2 = send(pair_1, y_up)
    up_two, down_two = send(below[0], z_up), send(above[0], z_down)
    up_two, down_two, near, distant, pair_2 = both(up_two, down_two, near, distant, pair_2)
    pair_3 = send(pair_2, y_up)
    p_all = line_up(spot, own, above, below, up_two, down_two)
    near_2, distant_2 = send(near, other_core), send(distant, other_core)
    w_part = w_products(p_all, near, distant)
    w_part = w_products(p_all, near_2, distant_2, w_part)
    w_part, *pairs = both(w_part, pair, pair_1, pair_2, pair_3)
    pairs += [send(p, other_core) for p in pairs]
    w_parts = lax.all_to_all(w_part, AXES, 0, 0, axis_index_groups=W_GROUPS, tiled=True)
    c_part = c_products(w_parts, pairs).astype(jnp.float16)
    return unpack(lax.all_to_all(c_part, AXES, 0, 0, axis_index_groups=C_GROUPS, tiled=True))


def solution(mesh):
    placed = (P("row", "col"),) * 4
    return jax.shard_map(
        local, mesh=mesh, in_specs=placed, out_specs=P("row", "col"), check_vma=False
    )
```

```python
import functools

import jax
import jax.numpy as jnp
from jax import lax
from jax.experimental import pallas as pl
from jax.experimental.pallas import tpu as pltpu
from jax.sharding import PartitionSpec as P

BLOCK = 128
AXES = ("row", "col")
PLANES, LANES = 8, 4


def place(z, xl, y, xh, k):
    return (2 * (z % PLANES) + xl) * 16 + 4 * (y % LANES) + 2 * xh + k


SPOTS = [
    (z, xl, y, xh, k)
    for z in range(PLANES)
    for xl in range(2)
    for y in range(LANES)
    for xh in range(2)
    for k in range(2)
]


def send(value, target):
    pairs = [(place(*spot), place(*target(*spot))) for spot in SPOTS]
    return lax.ppermute(value, AXES, pairs)


def turn(z, xl, y, xh, k):
    shift = (y - z // 2) % LANES
    return (z + shift if z % 2 else z - shift), xl, z // 2, xh, k


def turn_far(z, xl, y, xh, k):
    z_to, *rest = turn(z, xl, y, xh, k)
    return z_to + PLANES // 2, *rest


def z_up(z, xl, y, xh, k):
    return z + 1, xl, y, xh, k


def z_down(z, xl, y, xh, k):
    return z - 1, xl, y, xh, k


def y_up(z, xl, y, xh, k):
    return z, xl, y + 1, xh, k


def y_down(z, xl, y, xh, k):
    return z, xl, y - 1, xh, k


def far_x(z, xl, y, xh, k):
    return z, xl, y, 1 - xh, k


def other_core(z, xl, y, xh, k):
    return z, xl, y, xh, 1 - k


def swap(z, xl, y, xh, k):
    return z, k, y, xh, xl


def swap_far(z, xl, y, xh, k):
    return z, k, y, 1 - xh, xl


W_GROUPS = [
    [place(z, s ^ k, y, xh, k) for s in range(2) for y in range(LANES)]
    for z in range(PLANES)
    for xh in range(2)
    for k in range(2)
]


def coarse_row(y, xh, k, dk, dy, dx):
    i = 4 * ((y - dy) % LANES) + 2 * (xh ^ dx) + (k ^ dk)
    return i // 2, i % 2


C_GROUPS = [
    [
        place(*coarse_row(y, xh, k, dk, dy, dx), y, xh, k)
        for dk in range(2)
        for dy in range(LANES)
        for dx in range(2)
    ]
    for y in range(LANES)
    for xh in range(2)
    for k in range(2)
]


VMEM = pl.BlockSpec(memory_space=pltpu.VMEM)
SMEM = pl.BlockSpec(memory_space=pltpu.SMEM)
ANY = pl.BlockSpec(memory_space=pl.ANY)


def on_device(kernel, shape, dtype, specs, scratch=(), cost=None, grant=1):
    return pl.pallas_call(
        kernel,
        out_shape=jax.ShapeDtypeStruct(shape, dtype),
        in_specs=specs,
        out_specs=VMEM,
        scratch_shapes=scratch,
        compiler_params=pltpu.CompilerParams(vmem_limit_bytes=grant << 20),
        cost_estimate=cost,
    )


def dot32(a, b):
    return jnp.dot(a, b, preferred_element_type=jnp.float32)


def mask_kernel(p_any, a_any, p_pattern, a_pattern, p_out, a_out, p_stored, a_stored, sems):
    moves = [(p_pattern, p_stored), (p_any, p_out), (a_pattern, a_stored), (a_any, a_out)]
    copies = [pltpu.make_async_copy(*move, sems.at[i]) for i, move in enumerate(moves)]
    for copy in copies:
        copy.start()
    for first, stored, out_ref in ((0, p_stored, p_out), (2, a_stored, a_out)):
        copies[first].wait()
        copies[first + 1].wait()
        for i in range(out_ref.shape[0] // BLOCK):
            rows = slice(i * BLOCK, (i + 1) * BLOCK)
            for j in range(out_ref.shape[1] // BLOCK):
                columns = slice(j * BLOCK, (j + 1) * BLOCK)
                kept = stored[:, i : i + 1] if first == 0 else stored[i : i + 1, j : j + 1]
                kept = jnp.broadcast_to(kept.astype(jnp.float32), (BLOCK, BLOCK))
                out_ref[rows, columns] = out_ref[rows, columns] * kept.astype(out_ref.dtype)


def masked(prolong, a_matrix, p_pattern, a_pattern):
    return pl.pallas_call(
        mask_kernel,
        out_shape=[jax.ShapeDtypeStruct(v.shape, v.dtype) for v in (prolong, a_matrix)],
        in_specs=[ANY] * 4,
        out_specs=[VMEM, VMEM],
        scratch_shapes=[
            pltpu.VMEM(p_pattern.shape[::-1], p_pattern.dtype),
            pltpu.VMEM(a_pattern.shape, a_pattern.dtype),
            pltpu.SemaphoreType.DMA((4,)),
        ],
        compiler_params=pltpu.CompilerParams(vmem_limit_bytes=61 << 20),
        cost_estimate=pl.CostEstimate(flops=a_matrix.size, bytes_accessed=4 << 20, transcendentals=0),
    )(prolong, a_matrix, p_pattern.T, a_pattern)


def pair_kernel(one, two, out_ref):
    out_ref[0] = one[...]
    out_ref[1] = two[...]


def paired(one, two):
    cost = pl.CostEstimate(flops=0, bytes_accessed=8 * one.size, transcendentals=0)
    return on_device(pair_kernel, (2, *one.shape), one.dtype, [VMEM] * 2, cost=cost)(one, two)


def line_up_kernel(spot_ref, own, above, below, up_two, down_two, p_ref):
    z, y, xh = spot_ref[0], spot_ref[1], spot_ref[2]
    blocks = [own.at[0], above.at[0], down_two, below.at[1], own.at[1], above.at[1], up_two, below.at[0]]
    for d, block in enumerate(blocks):
        place_in = lax.rem(z + d - 2 * y - 1 + 2 * PLANES, PLANES)
        odd = (place_in < LANES).astype(jnp.int32)
        shift = jnp.where(odd == 1, place_in, PLANES - 1 - place_in)
        side = lax.rem(odd + xh, 2)
        column = pl.multiple_of(lax.rem(y + shift, LANES) * BLOCK, BLOCK)
        p_ref[side, :, pl.ds(column, BLOCK)] = block[...]


def line_up(spot, *blocks):
    size = blocks[0].shape[1]
    return on_device(
        line_up_kernel, (2, size, LANES * BLOCK), jnp.bfloat16, [SMEM] + [VMEM] * len(blocks),
        cost=pl.CostEstimate(flops=0, bytes_accessed=4 << 20, transcendentals=0),
    )(spot, *blocks)


def w_kernel(base, p_ref, one, two, *rest):
    out_ref = rest[-1]
    if base:
        out_ref[:base] = rest[0][...]
    size = one.shape[0]
    step = size // 3
    for c in range(0, LANES, 2):
        columns = slice(c * BLOCK, (c + 2) * BLOCK)
        for start in range(0, size, step):
            rows = slice(start, start + step)
            total = dot32(one[rows], p_ref[0, :, columns]) + dot32(two[rows], p_ref[1, :, columns])
            total = total.astype(jnp.bfloat16)
            out_ref[base + c, rows] = total[:, :BLOCK]
            out_ref[base + c + 1, rows] = total[:, BLOCK:]


def w_products(p_all, one, two, *before):
    size = one.shape[0]
    return on_device(
        functools.partial(w_kernel, LANES * len(before)),
        (LANES * (1 + len(before)), size, BLOCK),
        jnp.bfloat16,
        [VMEM] * (3 + len(before)),
        cost=pl.CostEstimate(flops=4 * size * size * LANES * BLOCK, bytes_accessed=6 << 20, transcendentals=0),
        grant=3,
    )(p_all, one, two, *before)


def c_kernel(parts_ref, *refs):
    pairs, (out_ref, w_ref) = refs[: 2 * LANES], refs[2 * LANES :]
    for start in range(0, parts_ref.shape[1], BLOCK):
        rows = slice(start, start + BLOCK)
        w = parts_ref[0, rows].astype(jnp.float32)
        for i in range(1, parts_ref.shape[0]):
            w += parts_ref[i, rows].astype(jnp.float32)
        turned = w.T
        high = turned.astype(jnp.bfloat16)
        w_ref[:BLOCK, rows] = high
        w_ref[BLOCK:, rows] = (turned - high.astype(jnp.float32)).astype(jnp.bfloat16)
    units = [pair.at[i] for pair in pairs for i in range(2)]
    top = jnp.zeros((BLOCK, BLOCK), jnp.float32)
    for i, unit in enumerate(units):
        both = dot32(w_ref[...], unit[...])
        part = both[:BLOCK] + both[BLOCK:]
        out_ref[i, :BLOCK] = part
        top = jnp.maximum(top, jnp.abs(part))
    top = jnp.max(jnp.max(top, axis=0, keepdims=True), axis=1, keepdims=True)
    power = jnp.ceil(jnp.log2(jnp.maximum(top, 1e-30))) - 14.0
    scale = jnp.exp2(-power)
    for i in range(len(units)):
        out_ref[i, :BLOCK] = out_ref[i, :BLOCK] * scale
        out_ref[i, BLOCK:] = jnp.broadcast_to(power, (8, BLOCK))


def c_products(parts, pairs):
    size = parts.shape[1]
    return on_device(
        c_kernel,
        (4 * LANES, BLOCK + 8, BLOCK),
        jnp.float32,
        [VMEM] * (2 * LANES + 1),
        [pltpu.VMEM((2 * BLOCK, size), jnp.bfloat16)],
        pl.CostEstimate(flops=16 * LANES * size * BLOCK * BLOCK, bytes_accessed=6 << 20, transcendentals=0),
        grant=2,
    )(parts, *pairs)


def unpack(parts):
    parts = parts.astype(jnp.float32)
    return jnp.sum(parts[:, :BLOCK] * jnp.exp2(parts[:, BLOCK : BLOCK + 1, :1]), axis=0).T


def both(*values):
    return lax.optimization_barrier(values)


def local(a_matrix, prolong, a_pattern, p_pattern):
    row, col = lax.axis_index("row"), lax.axis_index("col")
    spot = jnp.stack([row // 2, col // 4, (col // 2) % 2]).astype(jnp.int32)
    p_eff, a_eff = masked(prolong, a_matrix, p_pattern, a_pattern)
    first, second = send(p_eff, turn), send(p_eff, turn_far)
    across = send(p_eff, far_x)
    near, distant = send(a_eff, swap), send(a_eff, swap_far)
    pair = paired(p_eff, across)
    first, second, spot = both(first, second, spot)
    own = paired(first, second)
    below, above, pair_1 = both(send(own, z_up), send(own, z_down), send(pair, y_up))
    pair_2 = send(pair_1, y_up)
    up_two, down_two = send(below[0], z_up), send(above[0], z_down)
    up_two, down_two, near, distant, pair_2 = both(up_two, down_two, near, distant, pair_2)
    pair_3 = send(pair_2, y_up)
    p_all = line_up(spot, own, above, below, up_two, down_two)
    near_2, distant_2 = send(near, other_core), send(distant, other_core)
    w_part = w_products(p_all, near, distant)
    w_part = w_products(p_all, near_2, distant_2, w_part)
    w_part, *pairs = both(w_part, pair, pair_1, pair_2, pair_3)
    pairs += [send(p, other_core) for p in pairs]
    w_parts = lax.all_to_all(w_part, AXES, 0, 0, axis_index_groups=W_GROUPS, tiled=True)
    c_part = c_products(w_parts, pairs).astype(jnp.float16)
    return unpack(lax.all_to_all(c_part, AXES, 0, 0, axis_index_groups=C_GROUPS, tiled=True))


def solution(mesh):
    placed = (P("row", "col"),) * 4
    return jax.shard_map(
        local, mesh=mesh, in_specs=placed, out_specs=P("row", "col"), check_vma=False
    )
```

```python
import functools

import jax
import jax.numpy as jnp
from jax import lax
from jax.experimental import pallas as pl
from jax.experimental.pallas import tpu as pltpu
from jax.sharding import PartitionSpec as P

BLOCK = 128
AXES = ("row", "col")
PLANES, LANES = 8, 4


def place(z, xl, y, xh, k):
    return (2 * (z % PLANES) + xl) * 16 + 4 * (y % LANES) + 2 * xh + k


SPOTS = [
    (z, xl, y, xh, k)
    for z in range(PLANES)
    for xl in range(2)
    for y in range(LANES)
    for xh in range(2)
    for k in range(2)
]


def send(value, target):
    pairs = [(place(*spot), place(*target(*spot))) for spot in SPOTS]
    return lax.ppermute(value, AXES, pairs)


def turn(z, xl, y, xh, k):
    shift = (y - z // 2) % LANES
    return (z + shift if z % 2 else z - shift), xl, z // 2, xh, k


def turn_far(z, xl, y, xh, k):
    z_to, *rest = turn(z, xl, y, xh, k)
    return z_to + PLANES // 2, *rest


def z_up(z, xl, y, xh, k):
    return z + 1, xl, y, xh, k


def z_down(z, xl, y, xh, k):
    return z - 1, xl, y, xh, k


def y_up(z, xl, y, xh, k):
    return z, xl, y + 1, xh, k


def y_down(z, xl, y, xh, k):
    return z, xl, y - 1, xh, k


def far_x(z, xl, y, xh, k):
    return z, xl, y, 1 - xh, k


def other_core(z, xl, y, xh, k):
    return z, xl, y, xh, 1 - k


def swap(z, xl, y, xh, k):
    return z, k, y, xh, xl


def swap_far(z, xl, y, xh, k):
    return z, k, y, 1 - xh, xl


W_GROUPS = [
    [place(z, s ^ k, y, xh, k) for s in range(2) for y in range(LANES)]
    for z in range(PLANES)
    for xh in range(2)
    for k in range(2)
]


def coarse_row(y, xh, k, dk, dy, dx):
    i = 4 * ((y - dy) % LANES) + 2 * (xh ^ dx) + (k ^ dk)
    return i // 2, i % 2


C_GROUPS = [
    [
        place(*coarse_row(y, xh, k, dk, dy, dx), y, xh, k)
        for dk in range(2)
        for dy in range(LANES)
        for dx in range(2)
    ]
    for y in range(LANES)
    for xh in range(2)
    for k in range(2)
]


VMEM = pl.BlockSpec(memory_space=pltpu.VMEM)
SMEM = pl.BlockSpec(memory_space=pltpu.SMEM)
ANY = pl.BlockSpec(memory_space=pl.ANY)


def on_device(kernel, shape, dtype, specs, scratch=(), cost=None, grant=1):
    return pl.pallas_call(
        kernel,
        out_shape=jax.ShapeDtypeStruct(shape, dtype),
        in_specs=specs,
        out_specs=VMEM,
        scratch_shapes=scratch,
        compiler_params=pltpu.CompilerParams(vmem_limit_bytes=grant << 20),
        cost_estimate=cost,
    )


def dot32(a, b):
    return jnp.dot(a, b, preferred_element_type=jnp.float32)


def mask_kernel(p_any, a_any, p_pattern, a_pattern, p_out, a_out, p_stored, a_stored, sems):
    moves = [(p_pattern, p_stored), (p_any, p_out), (a_pattern, a_stored), (a_any, a_out)]
    copies = [pltpu.make_async_copy(*move, sems.at[i]) for i, move in enumerate(moves)]
    for copy in copies:
        copy.start()
    for first, stored, out_ref in ((0, p_stored, p_out), (2, a_stored, a_out)):
        copies[first].wait()
        copies[first + 1].wait()
        for i in range(out_ref.shape[0] // BLOCK):
            rows = slice(i * BLOCK, (i + 1) * BLOCK)
            for j in range(out_ref.shape[1] // BLOCK):
                columns = slice(j * BLOCK, (j + 1) * BLOCK)
                kept = stored[:, i : i + 1] if first == 0 else stored[i : i + 1, j : j + 1]
                kept = jnp.broadcast_to(kept.astype(jnp.float32), (BLOCK, BLOCK))
                out_ref[rows, columns] = out_ref[rows, columns] * kept.astype(out_ref.dtype)


def masked(prolong, a_matrix, p_pattern, a_pattern):
    return pl.pallas_call(
        mask_kernel,
        out_shape=[jax.ShapeDtypeStruct(v.shape, v.dtype) for v in (prolong, a_matrix)],
        in_specs=[ANY] * 4,
        out_specs=[VMEM, VMEM],
        scratch_shapes=[
            pltpu.VMEM(p_pattern.shape[::-1], p_pattern.dtype),
            pltpu.VMEM(a_pattern.shape, a_pattern.dtype),
            pltpu.SemaphoreType.DMA((4,)),
        ],
        compiler_params=pltpu.CompilerParams(vmem_limit_bytes=61 << 20),
        cost_estimate=pl.CostEstimate(flops=a_matrix.size, bytes_accessed=4 << 20, transcendentals=0),
    )(prolong, a_matrix, p_pattern.T, a_pattern)


def pair_kernel(one, two, out_ref):
    out_ref[0] = one[...]
    out_ref[1] = two[...]


def paired(one, two):
    cost = pl.CostEstimate(flops=0, bytes_accessed=8 * one.size, transcendentals=0)
    return on_device(pair_kernel, (2, *one.shape), one.dtype, [VMEM] * 2, cost=cost)(one, two)


def line_up_kernel(spot_ref, own, above, below, up_two, down_two, p_ref):
    z, y, xh = spot_ref[0], spot_ref[1], spot_ref[2]
    blocks = [own.at[0], above.at[0], down_two, below.at[1], own.at[1], above.at[1], up_two, below.at[0]]
    for d, block in enumerate(blocks):
        place_in = lax.rem(z + d - 2 * y - 1 + 2 * PLANES, PLANES)
        odd = (place_in < LANES).astype(jnp.int32)
        shift = jnp.where(odd == 1, place_in, PLANES - 1 - place_in)
        side = lax.rem(odd + xh, 2)
        column = pl.multiple_of(lax.rem(y + shift, LANES) * BLOCK, BLOCK)
        p_ref[side, :, pl.ds(column, BLOCK)] = block[...]


def line_up(spot, *blocks):
    size = blocks[0].shape[1]
    return on_device(
        line_up_kernel, (2, size, LANES * BLOCK), jnp.bfloat16, [SMEM] + [VMEM] * len(blocks),
        cost=pl.CostEstimate(flops=0, bytes_accessed=4 << 20, transcendentals=0),
    )(spot, *blocks)


def w_kernel(base, p_ref, one, two, *rest):
    out_ref = rest[-1]
    if base:
        out_ref[:base] = rest[0][...]
    size = one.shape[0]
    step = size // 3
    for c in range(0, LANES, 2):
        columns = slice(c * BLOCK, (c + 2) * BLOCK)
        for start in range(0, size, step):
            rows = slice(start, start + step)
            total = dot32(one[rows], p_ref[0, :, columns]) + dot32(two[rows], p_ref[1, :, columns])
            total = total.astype(jnp.bfloat16)
            out_ref[base + c, rows] = total[:, :BLOCK]
            out_ref[base + c + 1, rows] = total[:, BLOCK:]


def w_products(p_all, one, two, *before):
    size = one.shape[0]
    return on_device(
        functools.partial(w_kernel, LANES * len(before)),
        (LANES * (1 + len(before)), size, BLOCK),
        jnp.bfloat16,
        [VMEM] * (3 + len(before)),
        cost=pl.CostEstimate(flops=4 * size * size * LANES * BLOCK, bytes_accessed=6 << 20, transcendentals=0),
        grant=3,
    )(p_all, one, two, *before)


def c_kernel(parts_ref, *refs):
    pairs, (out_ref, w_ref) = refs[: 2 * LANES], refs[2 * LANES :]
    for start in range(0, parts_ref.shape[1], BLOCK):
        rows = slice(start, start + BLOCK)
        w = parts_ref[0, rows].astype(jnp.float32)
        for i in range(1, parts_ref.shape[0]):
            w += parts_ref[i, rows].astype(jnp.float32)
        turned = w.T
        high = turned.astype(jnp.bfloat16)
        w_ref[:BLOCK, rows] = high
        w_ref[BLOCK:, rows] = (turned - high.astype(jnp.float32)).astype(jnp.bfloat16)
    units = [pair.at[i] for pair in pairs for i in range(2)]
    top = jnp.zeros((BLOCK, BLOCK), jnp.float32)
    for i, unit in enumerate(units):
        both = dot32(w_ref[...], unit[...])
        part = both[:BLOCK] + both[BLOCK:]
        out_ref[i, :BLOCK] = part
        top = jnp.maximum(top, jnp.abs(part))
    top = jnp.max(jnp.max(top, axis=0, keepdims=True), axis=1, keepdims=True)
    power = jnp.ceil(jnp.log2(jnp.maximum(top, 1e-30))) - 14.0
    scale = jnp.exp2(-power)
    for i in range(len(units)):
        out_ref[i, :BLOCK] = out_ref[i, :BLOCK] * scale
        out_ref[i, BLOCK:] = jnp.broadcast_to(power, (8, BLOCK))


def c_products(parts, pairs):
    size = parts.shape[1]
    return on_device(
        c_kernel,
        (4 * LANES, BLOCK + 8, BLOCK),
        jnp.float32,
        [VMEM] * (2 * LANES + 1),
        [pltpu.VMEM((2 * BLOCK, size), jnp.bfloat16)],
        pl.CostEstimate(flops=16 * LANES * size * BLOCK * BLOCK, bytes_accessed=6 << 20, transcendentals=0),
        grant=2,
    )(parts, *pairs)


def unpack(parts):
    parts = parts.astype(jnp.float32)
    return jnp.sum(parts[:, :BLOCK] * jnp.exp2(parts[:, BLOCK : BLOCK + 1, :1]), axis=0).T


def both(*values):
    return lax.optimization_barrier(values)


def local(a_matrix, prolong, a_pattern, p_pattern):
    row, col = lax.axis_index("row"), lax.axis_index("col")
    spot = jnp.stack([row // 2, col // 4, (col // 2) % 2]).astype(jnp.int32)
    p_eff, a_eff = masked(prolong, a_matrix, p_pattern, a_pattern)
    first, second = send(p_eff, turn), send(p_eff, turn_far)
    across = send(p_eff, far_x)
    near, distant = send(a_eff, swap), send(a_eff, swap_far)
    pair = paired(p_eff, across)
    first, second, spot, pair = both(first, second, spot, pair)
    own = paired(first, second)
    below, above, pair_1 = both(send(own, z_up), send(own, z_down), send(pair, y_up))
    pair_3 = send(pair, y_down)
    up_two, down_two = send(below[0], z_up), send(above[0], z_down)
    up_two, down_two, near, distant, pair_3, pair_1 = both(up_two, down_two, near, distant, pair_3, pair_1)
    beyond = send(pair_1[0], y_up), send(pair_3[1], y_down)
    p_all = line_up(spot, own, above, below, up_two, down_two)
    near_2, distant_2 = send(near, other_core), send(distant, other_core)
    w_part = w_products(p_all, near, distant)
    w_part = w_products(p_all, near_2, distant_2, w_part)
    w_part, *pairs = both(w_part, pair, pair_1, paired(*beyond), pair_3)
    pairs += [send(p, other_core) for p in pairs]
    w_parts = lax.all_to_all(w_part, AXES, 0, 0, axis_index_groups=W_GROUPS, tiled=True)
    c_part = c_products(w_parts, pairs).astype(jnp.float16)
    return unpack(lax.all_to_all(c_part, AXES, 0, 0, axis_index_groups=C_GROUPS, tiled=True))


def solution(mesh):
    placed = (P("row", "col"),) * 4
    return jax.shard_map(
        local, mesh=mesh, in_specs=placed, out_specs=P("row", "col"), check_vma=False
    )
```

```python
import functools

import jax
import jax.numpy as jnp
from jax import lax
from jax.experimental import pallas as pl
from jax.experimental.pallas import tpu as pltpu
from jax.sharding import PartitionSpec as P

BLOCK = 128
AXES = ("row", "col")
PLANES, LANES = 8, 4


def place(z, xl, y, xh, k):
    return (2 * (z % PLANES) + xl) * 16 + 4 * (y % LANES) + 2 * xh + k


SPOTS = [
    (z, xl, y, xh, k)
    for z in range(PLANES)
    for xl in range(2)
    for y in range(LANES)
    for xh in range(2)
    for k in range(2)
]


def send(value, target):
    pairs = [(place(*spot), place(*target(*spot))) for spot in SPOTS]
    return lax.ppermute(value, AXES, pairs)


def turn(z, xl, y, xh, k):
    shift = (y - z // 2) % LANES
    return (z + shift if z % 2 else z - shift), xl, z // 2, xh, k


def turn_far(z, xl, y, xh, k):
    z_to, *rest = turn(z, xl, y, xh, k)
    return z_to + PLANES // 2, *rest


def z_up(z, xl, y, xh, k):
    return z + 1, xl, y, xh, k


def z_down(z, xl, y, xh, k):
    return z - 1, xl, y, xh, k


def y_up(z, xl, y, xh, k):
    return z, xl, y + 1, xh, k


def y_down(z, xl, y, xh, k):
    return z, xl, y - 1, xh, k


def far_x(z, xl, y, xh, k):
    return z, xl, y, 1 - xh, k


def other_core(z, xl, y, xh, k):
    return z, xl, y, xh, 1 - k


def swap(z, xl, y, xh, k):
    return z, k, y, xh, xl


def swap_far(z, xl, y, xh, k):
    return z, k, y, 1 - xh, xl


W_GROUPS = [
    [place(z, s ^ k, y, xh, k) for s in range(2) for y in range(LANES)]
    for z in range(PLANES)
    for xh in range(2)
    for k in range(2)
]


def coarse_row(y, xh, k, dk, dy, dx):
    i = 4 * ((y - dy) % LANES) + 2 * (xh ^ dx) + (k ^ dk)
    return i // 2, i % 2


C_GROUPS = [
    [
        place(*coarse_row(y, xh, k, dk, dy, dx), y, xh, k)
        for dk in range(2)
        for dy in range(LANES)
        for dx in range(2)
    ]
    for y in range(LANES)
    for xh in range(2)
    for k in range(2)
]


VMEM = pl.BlockSpec(memory_space=pltpu.VMEM)
SMEM = pl.BlockSpec(memory_space=pltpu.SMEM)
ANY = pl.BlockSpec(memory_space=pl.ANY)


def on_device(kernel, shape, dtype, specs, scratch=(), cost=None, grant=1):
    return pl.pallas_call(
        kernel,
        out_shape=jax.ShapeDtypeStruct(shape, dtype),
        in_specs=specs,
        out_specs=VMEM,
        scratch_shapes=scratch,
        compiler_params=pltpu.CompilerParams(vmem_limit_bytes=grant << 20),
        cost_estimate=cost,
    )


def dot32(a, b):
    return jnp.dot(a, b, preferred_element_type=jnp.float32)


def mask_kernel(p_any, a_any, p_pattern, a_pattern, p_out, a_out, p_stored, a_stored, sems):
    moves = [(p_pattern, p_stored), (p_any, p_out), (a_pattern, a_stored), (a_any, a_out)]
    copies = [pltpu.make_async_copy(*move, sems.at[i]) for i, move in enumerate(moves)]
    for copy in copies:
        copy.start()
    for first, stored, out_ref in ((0, p_stored, p_out), (2, a_stored, a_out)):
        copies[first].wait()
        copies[first + 1].wait()
        for i in range(out_ref.shape[0] // BLOCK):
            rows = slice(i * BLOCK, (i + 1) * BLOCK)
            for j in range(out_ref.shape[1] // BLOCK):
                columns = slice(j * BLOCK, (j + 1) * BLOCK)
                kept = stored[:, i : i + 1] if first == 0 else stored[i : i + 1, j : j + 1]
                kept = jnp.broadcast_to(kept.astype(jnp.float32), (BLOCK, BLOCK))
                out_ref[rows, columns] = out_ref[rows, columns] * kept.astype(out_ref.dtype)


def masked(prolong, a_matrix, p_pattern, a_pattern):
    return pl.pallas_call(
        mask_kernel,
        out_shape=[jax.ShapeDtypeStruct(v.shape, v.dtype) for v in (prolong, a_matrix)],
        in_specs=[ANY] * 4,
        out_specs=[VMEM, VMEM],
        scratch_shapes=[
            pltpu.VMEM(p_pattern.shape[::-1], p_pattern.dtype),
            pltpu.VMEM(a_pattern.shape, a_pattern.dtype),
            pltpu.SemaphoreType.DMA((4,)),
        ],
        compiler_params=pltpu.CompilerParams(vmem_limit_bytes=61 << 20),
        cost_estimate=pl.CostEstimate(flops=a_matrix.size, bytes_accessed=4 << 20, transcendentals=0),
    )(prolong, a_matrix, p_pattern.T, a_pattern)


def pair_kernel(one, two, out_ref):
    out_ref[0] = one[...]
    out_ref[1] = two[...]


def paired(one, two):
    cost = pl.CostEstimate(flops=0, bytes_accessed=8 * one.size, transcendentals=0)
    return on_device(pair_kernel, (2, *one.shape), one.dtype, [VMEM] * 2, cost=cost)(one, two)


def line_up_kernel(spot_ref, own, above, below, up_two, down_two, p_ref):
    z, y, xh = spot_ref[0], spot_ref[1], spot_ref[2]
    blocks = [own.at[0], above.at[0], down_two, below.at[1], own.at[1], above.at[1], up_two, below.at[0]]
    for d, block in enumerate(blocks):
        place_in = lax.rem(z + d - 2 * y - 1 + 2 * PLANES, PLANES)
        odd = (place_in < LANES).astype(jnp.int32)
        shift = jnp.where(odd == 1, place_in, PLANES - 1 - place_in)
        side = lax.rem(odd + xh, 2)
        column = pl.multiple_of(lax.rem(y + shift, LANES) * BLOCK, BLOCK)
        p_ref[side, :, pl.ds(column, BLOCK)] = block[...]


def line_up(spot, *blocks):
    size = blocks[0].shape[1]
    return on_device(
        line_up_kernel, (2, size, LANES * BLOCK), jnp.bfloat16, [SMEM] + [VMEM] * len(blocks),
        cost=pl.CostEstimate(flops=0, bytes_accessed=4 << 20, transcendentals=0),
    )(spot, *blocks)


def w_kernel(base, p_ref, one, two, *rest):
    out_ref = rest[-1]
    if base:
        out_ref[:base] = rest[0][...]
    size = one.shape[0]
    step = size // 3
    for c in range(0, LANES, 2):
        columns = slice(c * BLOCK, (c + 2) * BLOCK)
        for start in range(0, size, step):
            rows = slice(start, start + step)
            total = dot32(one[rows], p_ref[0, :, columns]) + dot32(two[rows], p_ref[1, :, columns])
            total = total.astype(jnp.bfloat16)
            out_ref[base + c, rows] = total[:, :BLOCK]
            out_ref[base + c + 1, rows] = total[:, BLOCK:]


def w_products(p_all, one, two, *before):
    size = one.shape[0]
    return on_device(
        functools.partial(w_kernel, LANES * len(before)),
        (LANES * (1 + len(before)), size, BLOCK),
        jnp.bfloat16,
        [VMEM] * (3 + len(before)),
        cost=pl.CostEstimate(flops=4 * size * size * LANES * BLOCK, bytes_accessed=6 << 20, transcendentals=0),
        grant=3,
    )(p_all, one, two, *before)


def c_kernel(parts_ref, *refs):
    pairs, (out_ref, w_ref) = refs[: 2 * LANES], refs[2 * LANES :]
    for start in range(0, parts_ref.shape[1], BLOCK):
        rows = slice(start, start + BLOCK)
        w = parts_ref[0, rows].astype(jnp.float32)
        for i in range(1, parts_ref.shape[0]):
            w += parts_ref[i, rows].astype(jnp.float32)
        turned = w.T
        high = turned.astype(jnp.bfloat16)
        w_ref[:BLOCK, rows] = high
        w_ref[BLOCK:, rows] = (turned - high.astype(jnp.float32)).astype(jnp.bfloat16)
    units = [pair.at[i] for pair in pairs for i in range(2)]
    top = jnp.zeros((BLOCK, BLOCK), jnp.float32)
    for i, unit in enumerate(units):
        both = dot32(w_ref[...], unit[...])
        part = both[:BLOCK] + both[BLOCK:]
        out_ref[i, :BLOCK] = part
        top = jnp.maximum(top, jnp.abs(part))
    top = jnp.max(jnp.max(top, axis=0, keepdims=True), axis=1, keepdims=True)
    power = jnp.ceil(jnp.log2(jnp.maximum(top, 1e-30))) - 14.0
    scale = jnp.exp2(-power)
    for i in range(len(units)):
        out_ref[i, :BLOCK] = out_ref[i, :BLOCK] * scale
        out_ref[i, BLOCK:] = jnp.broadcast_to(power, (8, BLOCK))


def c_products(parts, pairs):
    size = parts.shape[1]
    return on_device(
        c_kernel,
        (4 * LANES, BLOCK + 8, BLOCK),
        jnp.float32,
        [VMEM] * (2 * LANES + 1),
        [pltpu.VMEM((2 * BLOCK, size), jnp.bfloat16)],
        pl.CostEstimate(flops=16 * LANES * size * BLOCK * BLOCK, bytes_accessed=6 << 20, transcendentals=0),
        grant=2,
    )(parts, *pairs)


def unpack(parts):
    parts = parts.astype(jnp.float32)
    return jnp.sum(parts[:, :BLOCK] * jnp.exp2(parts[:, BLOCK : BLOCK + 1, :1]), axis=0).T


def both(*values):
    return lax.optimization_barrier(values)


def local(a_matrix, prolong, a_pattern, p_pattern):
    row, col = lax.axis_index("row"), lax.axis_index("col")
    spot = jnp.stack([row // 2, col // 4, (col // 2) % 2]).astype(jnp.int32)
    p_eff, a_eff = masked(prolong, a_matrix, p_pattern, a_pattern)
    first, second = send(p_eff, turn), send(p_eff, turn_far)
    across = send(p_eff, far_x)
    near, distant = send(a_eff, swap), send(a_eff, swap_far)
    pair = paired(p_eff, across)
    first, second, spot = both(first, second, spot)
    own = paired(first, second)
    below, above, pair_1 = both(send(own, z_up), send(own, z_down), send(pair, y_up))
    pair_3 = send(pair, y_down)
    up_two, down_two = send(below[0], z_up), send(above[0], z_down)
    up_two, down_two, near, distant, pair_3, pair_1 = both(up_two, down_two, near, distant, pair_3, pair_1)
    beyond = send(pair_1[0], y_up), send(pair_3[1], y_down)
    p_all = line_up(spot, own, above, below, up_two, down_two)
    near_2, distant_2 = send(near, other_core), send(distant, other_core)
    w_part = w_products(p_all, near, distant)
    w_part = w_products(p_all, near_2, distant_2, w_part)
    w_part, pair, pair_1, pair_3, *beyond = both(w_part, pair, pair_1, pair_3, *beyond)
    pairs = [pair, pair_1, paired(*beyond), pair_3]
    pairs += [send(p, other_core) for p in pairs]
    w_parts = lax.all_to_all(w_part, AXES, 0, 0, axis_index_groups=W_GROUPS, tiled=True)
    c_part = c_products(w_parts, pairs).astype(jnp.float16)
    return unpack(lax.all_to_all(c_part, AXES, 0, 0, axis_index_groups=C_GROUPS, tiled=True))


def solution(mesh):
    placed = (P("row", "col"),) * 4
    return jax.shard_map(
        local, mesh=mesh, in_specs=placed, out_specs=P("row", "col"), check_vma=False
    )
```

```python
import functools

import jax
import jax.numpy as jnp
from jax import lax
from jax.experimental import pallas as pl
from jax.experimental.pallas import tpu as pltpu
from jax.sharding import PartitionSpec as P

BLOCK = 128
AXES = ("row", "col")
PLANES, LANES = 8, 4


def place(z, xl, y, xh, k):
    return (2 * (z % PLANES) + xl) * 16 + 4 * (y % LANES) + 2 * xh + k


SPOTS = [
    (z, xl, y, xh, k)
    for z in range(PLANES)
    for xl in range(2)
    for y in range(LANES)
    for xh in range(2)
    for k in range(2)
]


def send(value, target):
    pairs = [(place(*spot), place(*target(*spot))) for spot in SPOTS]
    return lax.ppermute(value, AXES, pairs)


def turn(z, xl, y, xh, k):
    shift = (y - z // 2) % LANES
    return (z + shift if z % 2 else z - shift), xl, z // 2, xh, k


def turn_far(z, xl, y, xh, k):
    z_to, *rest = turn(z, xl, y, xh, k)
    return z_to + PLANES // 2, *rest


def z_up(z, xl, y, xh, k):
    return z + 1, xl, y, xh, k


def z_down(z, xl, y, xh, k):
    return z - 1, xl, y, xh, k


def y_up(z, xl, y, xh, k):
    return z, xl, y + 1, xh, k


def y_down(z, xl, y, xh, k):
    return z, xl, y - 1, xh, k


def far_x(z, xl, y, xh, k):
    return z, xl, y, 1 - xh, k


def other_core(z, xl, y, xh, k):
    return z, xl, y, xh, 1 - k


def swap(z, xl, y, xh, k):
    return z, k, y, xh, xl


def swap_far(z, xl, y, xh, k):
    return z, k, y, 1 - xh, xl


W_GROUPS = [
    [place(z, s ^ k, y, xh, k) for s in range(2) for y in range(LANES)]
    for z in range(PLANES)
    for xh in range(2)
    for k in range(2)
]


def coarse_row(y, xh, k, dk, dy, dx):
    i = 4 * ((y - dy) % LANES) + 2 * (xh ^ dx) + (k ^ dk)
    return i // 2, i % 2


C_GROUPS = [
    [
        place(*coarse_row(y, xh, k, dk, dy, dx), y, xh, k)
        for dk in range(2)
        for dy in range(LANES)
        for dx in range(2)
    ]
    for y in range(LANES)
    for xh in range(2)
    for k in range(2)
]


VMEM = pl.BlockSpec(memory_space=pltpu.VMEM)
SMEM = pl.BlockSpec(memory_space=pltpu.SMEM)
ANY = pl.BlockSpec(memory_space=pl.ANY)


def on_device(kernel, shape, dtype, specs, scratch=(), cost=None, grant=0.25):
    return pl.pallas_call(
        kernel,
        out_shape=jax.ShapeDtypeStruct(shape, dtype),
        in_specs=specs,
        out_specs=VMEM,
        scratch_shapes=scratch,
        compiler_params=pltpu.CompilerParams(vmem_limit_bytes=int(grant * 2**20)),
        cost_estimate=cost,
    )


def dot32(a, b):
    return jnp.dot(a, b, preferred_element_type=jnp.float32)


def mask_kernel(p_any, a_any, p_pattern, a_pattern, p_out, a_out, p_stored, a_stored, sems):
    moves = [(p_pattern, p_stored), (p_any, p_out), (a_pattern, a_stored), (a_any, a_out)]
    copies = [pltpu.make_async_copy(*move, sems.at[i]) for i, move in enumerate(moves)]
    for copy in copies:
        copy.start()
    for first, stored, out_ref in ((0, p_stored, p_out), (2, a_stored, a_out)):
        copies[first].wait()
        copies[first + 1].wait()
        for i in range(out_ref.shape[0] // BLOCK):
            rows = slice(i * BLOCK, (i + 1) * BLOCK)
            for j in range(out_ref.shape[1] // BLOCK):
                columns = slice(j * BLOCK, (j + 1) * BLOCK)
                kept = stored[:, i : i + 1] if first == 0 else stored[i : i + 1, j : j + 1]
                kept = jnp.broadcast_to(kept.astype(jnp.float32), (BLOCK, BLOCK))
                out_ref[rows, columns] = out_ref[rows, columns] * kept.astype(out_ref.dtype)


def masked(prolong, a_matrix, p_pattern, a_pattern):
    return pl.pallas_call(
        mask_kernel,
        out_shape=[jax.ShapeDtypeStruct(v.shape, v.dtype) for v in (prolong, a_matrix)],
        in_specs=[ANY] * 4,
        out_specs=[VMEM, VMEM],
        scratch_shapes=[
            pltpu.VMEM(p_pattern.shape[::-1], p_pattern.dtype),
            pltpu.VMEM(a_pattern.shape, a_pattern.dtype),
            pltpu.SemaphoreType.DMA((4,)),
        ],
        compiler_params=pltpu.CompilerParams(vmem_limit_bytes=61 << 20),
        cost_estimate=pl.CostEstimate(flops=a_matrix.size, bytes_accessed=4 << 20, transcendentals=0),
    )(prolong, a_matrix, p_pattern.T, a_pattern)


def pair_kernel(one, two, out_ref):
    out_ref[0] = one[...]
    out_ref[1] = two[...]


def paired(one, two):
    cost = pl.CostEstimate(flops=0, bytes_accessed=8 * one.size, transcendentals=0)
    return on_device(pair_kernel, (2, *one.shape), one.dtype, [VMEM] * 2, cost=cost)(one, two)


def line_up_kernel(spot_ref, own, above, below, up_two, down_two, p_ref):
    z, y, xh = spot_ref[0], spot_ref[1], spot_ref[2]
    blocks = [own.at[0], above.at[0], down_two, below.at[1], own.at[1], above.at[1], up_two, below.at[0]]
    for d, block in enumerate(blocks):
        place_in = lax.rem(z + d - 2 * y - 1 + 2 * PLANES, PLANES)
        odd = (place_in < LANES).astype(jnp.int32)
        shift = jnp.where(odd == 1, place_in, PLANES - 1 - place_in)
        side = lax.rem(odd + xh, 2)
        column = pl.multiple_of(lax.rem(y + shift, LANES) * BLOCK, BLOCK)
        p_ref[side, :, pl.ds(column, BLOCK)] = block[...]


def line_up(spot, *blocks):
    size = blocks[0].shape[1]
    return on_device(
        line_up_kernel, (2, size, LANES * BLOCK), jnp.bfloat16, [SMEM] + [VMEM] * len(blocks),
        cost=pl.CostEstimate(flops=0, bytes_accessed=4 << 20, transcendentals=0),
    )(spot, *blocks)


def w_kernel(base, p_ref, one, two, *rest):
    out_ref = rest[-1]
    if base:
        out_ref[:base] = rest[0][...]
    size = one.shape[0]
    step = size // 3
    for c in range(0, LANES, 2):
        columns = slice(c * BLOCK, (c + 2) * BLOCK)
        for start in range(0, size, step):
            rows = slice(start, start + step)
            total = dot32(one[rows], p_ref[0, :, columns]) + dot32(two[rows], p_ref[1, :, columns])
            total = total.astype(jnp.bfloat16)
            out_ref[base + c, rows] = total[:, :BLOCK]
            out_ref[base + c + 1, rows] = total[:, BLOCK:]


def w_products(p_all, one, two, *before):
    size = one.shape[0]
    return on_device(
        functools.partial(w_kernel, LANES * len(before)),
        (LANES * (1 + len(before)), size, BLOCK),
        jnp.bfloat16,
        [VMEM] * (3 + len(before)),
        cost=pl.CostEstimate(flops=4 * size * size * LANES * BLOCK, bytes_accessed=6 << 20, transcendentals=0),
        grant=2,
    )(p_all, one, two, *before)


def coarse_chunks(w_ref, pairs, out_ref):
    units = [pair.at[i] for pair in pairs for i in range(2)]
    top = jnp.zeros((BLOCK, BLOCK), jnp.float32)
    for i, unit in enumerate(units):
        both = dot32(w_ref[...], unit[...])
        part = both[:BLOCK] + both[BLOCK:]
        out_ref[i, :BLOCK] = part
        top = jnp.maximum(top, jnp.abs(part))
    top = jnp.max(jnp.max(top, axis=0, keepdims=True), axis=1, keepdims=True)
    power = jnp.ceil(jnp.log2(jnp.maximum(top, 1e-30))) - 14.0
    scale = jnp.exp2(-power)
    for i in range(len(units)):
        out_ref[i, :BLOCK] = out_ref[i, :BLOCK] * scale
        out_ref[i, BLOCK:] = jnp.broadcast_to(power, (8, BLOCK))


def own_kernel(parts_ref, *refs):
    pairs, (out_ref, w_ref) = refs[:LANES], refs[LANES:]
    for start in range(0, parts_ref.shape[1], BLOCK):
        rows = slice(start, start + BLOCK)
        w = parts_ref[0, rows].astype(jnp.float32)
        for i in range(1, parts_ref.shape[0]):
            w += parts_ref[i, rows].astype(jnp.float32)
        turned = w.T
        high = turned.astype(jnp.bfloat16)
        w_ref[:BLOCK, rows] = high
        w_ref[BLOCK:, rows] = (turned - high.astype(jnp.float32)).astype(jnp.bfloat16)
    coarse_chunks(w_ref, pairs, out_ref)


def other_kernel(w_ref, *refs):
    coarse_chunks(w_ref, refs[:LANES], refs[LANES])


def c_products(parts, pairs):
    size = parts.shape[1]
    cost = pl.CostEstimate(flops=8 * LANES * size * BLOCK * BLOCK, bytes_accessed=4 << 20, transcendentals=0)
    chunks = jax.ShapeDtypeStruct((2 * LANES, BLOCK + 8, BLOCK), jnp.float32)
    own, w_both = pl.pallas_call(
        own_kernel,
        out_shape=[chunks, jax.ShapeDtypeStruct((2 * BLOCK, size), jnp.bfloat16)],
        in_specs=[VMEM] * (LANES + 1),
        out_specs=[VMEM] * 2,
        compiler_params=pltpu.CompilerParams(vmem_limit_bytes=2 << 20),
        cost_estimate=cost,
    )(parts, *pairs[:LANES])
    other = on_device(
        other_kernel, chunks.shape, chunks.dtype, [VMEM] * (LANES + 1), cost=cost, grant=2
    )(w_both, *pairs[LANES:])
    return jnp.concatenate([own, other])


def unpack(parts):
    parts = parts.astype(jnp.float32)
    return jnp.sum(parts[:, :BLOCK] * jnp.exp2(parts[:, BLOCK : BLOCK + 1, :1]), axis=0).T


def both(*values):
    return lax.optimization_barrier(values)


def local(a_matrix, prolong, a_pattern, p_pattern):
    row, col = lax.axis_index("row"), lax.axis_index("col")
    spot = jnp.stack([row // 2, col // 4, (col // 2) % 2]).astype(jnp.int32)
    p_eff, a_eff = masked(prolong, a_matrix, p_pattern, a_pattern)
    first, second = send(p_eff, turn), send(p_eff, turn_far)
    across = send(p_eff, far_x)
    near, distant = send(a_eff, swap), send(a_eff, swap_far)
    pair = paired(p_eff, across)
    first, second, spot = both(first, second, spot)
    own = paired(first, second)
    below, above, pair_1 = both(send(own, z_up), send(own, z_down), send(pair, y_up))
    pair_3 = send(pair, y_down)
    up_two, down_two = send(below[0], z_up), send(above[0], z_down)
    up_two, down_two, near, distant, pair_3, pair_1 = both(up_two, down_two, near, distant, pair_3, pair_1)
    beyond = send(pair_1[0], y_up), send(pair_3[1], y_down)
    p_all = line_up(spot, own, above, below, up_two, down_two)
    near_2, distant_2 = send(near, other_core), send(distant, other_core)
    w_part = w_products(p_all, near, distant)
    w_part = w_products(p_all, near_2, distant_2, w_part)
    w_part, pair, pair_1, pair_3, *beyond = both(w_part, pair, pair_1, pair_3, *beyond)
    pairs = [pair, pair_1, paired(*beyond), pair_3]
    pairs += [send(p, other_core) for p in pairs]
    w_parts = lax.all_to_all(w_part, AXES, 0, 0, axis_index_groups=W_GROUPS, tiled=True)
    c_part = c_products(w_parts, pairs).astype(jnp.float16)
    return unpack(lax.all_to_all(c_part, AXES, 0, 0, axis_index_groups=C_GROUPS, tiled=True))


def solution(mesh):
    placed = (P("row", "col"),) * 4
    return jax.shard_map(
        local, mesh=mesh, in_specs=placed, out_specs=P("row", "col"), check_vma=False
    )
```

```python
import functools

import jax
import jax.numpy as jnp
from jax import lax
from jax.experimental import pallas as pl
from jax.experimental.pallas import tpu as pltpu
from jax.sharding import PartitionSpec as P

BLOCK = 128
AXES = ("row", "col")
PLANES, LANES = 8, 4


def place(z, xl, y, xh, k):
    return (2 * (z % PLANES) + xl) * 16 + 4 * (y % LANES) + 2 * xh + k


SPOTS = [
    (z, xl, y, xh, k)
    for z in range(PLANES)
    for xl in range(2)
    for y in range(LANES)
    for xh in range(2)
    for k in range(2)
]


def send(value, target):
    pairs = [(place(*spot), place(*target(*spot))) for spot in SPOTS]
    return lax.ppermute(value, AXES, pairs)


def turn(z, xl, y, xh, k):
    shift = (y - z // 2) % LANES
    return (z + shift if z % 2 else z - shift), xl, z // 2, xh, k


def turn_far(z, xl, y, xh, k):
    z_to, *rest = turn(z, xl, y, xh, k)
    return z_to + PLANES // 2, *rest


def z_up(z, xl, y, xh, k):
    return z + 1, xl, y, xh, k


def z_down(z, xl, y, xh, k):
    return z - 1, xl, y, xh, k


def y_up(z, xl, y, xh, k):
    return z, xl, y + 1, xh, k


def y_down(z, xl, y, xh, k):
    return z, xl, y - 1, xh, k


def far_x(z, xl, y, xh, k):
    return z, xl, y, 1 - xh, k


def other_core(z, xl, y, xh, k):
    return z, xl, y, xh, 1 - k


def swap(z, xl, y, xh, k):
    return z, k, y, xh, xl


def swap_far(z, xl, y, xh, k):
    return z, k, y, 1 - xh, xl


W_GROUPS = [
    [place(z, s ^ k, y, xh, k) for s in range(2) for y in range(LANES)]
    for z in range(PLANES)
    for xh in range(2)
    for k in range(2)
]


def coarse_row(y, xh, k, dk, dy, dx):
    i = 4 * ((y - dy) % LANES) + 2 * (xh ^ dx) + (k ^ dk)
    return i // 2, i % 2


C_GROUPS = [
    [
        place(*coarse_row(y, xh, k, dk, dy, dx), y, xh, k)
        for dk in range(2)
        for dy in range(LANES)
        for dx in range(2)
    ]
    for y in range(LANES)
    for xh in range(2)
    for k in range(2)
]


VMEM = pl.BlockSpec(memory_space=pltpu.VMEM)
SMEM = pl.BlockSpec(memory_space=pltpu.SMEM)
ANY = pl.BlockSpec(memory_space=pl.ANY)


def on_device(kernel, shape, dtype, specs, scratch=(), cost=None, grant=0.25):
    return pl.pallas_call(
        kernel,
        out_shape=jax.ShapeDtypeStruct(shape, dtype),
        in_specs=specs,
        out_specs=VMEM,
        scratch_shapes=scratch,
        compiler_params=pltpu.CompilerParams(vmem_limit_bytes=int(grant * 2**20)),
        cost_estimate=cost,
    )


def dot32(a, b):
    return jnp.dot(a, b, preferred_element_type=jnp.float32)


def mask_kernel(p_any, a_any, p_pattern, a_pattern, p_out, a_out, p_stored, a_stored, sems):
    moves = [(p_pattern, p_stored), (p_any, p_out), (a_pattern, a_stored), (a_any, a_out)]
    copies = [pltpu.make_async_copy(*move, sems.at[i]) for i, move in enumerate(moves)]
    for copy in copies:
        copy.start()
    for first, stored, out_ref in ((0, p_stored, p_out), (2, a_stored, a_out)):
        copies[first].wait()
        copies[first + 1].wait()
        for i in range(out_ref.shape[0] // BLOCK):
            rows = slice(i * BLOCK, (i + 1) * BLOCK)
            for j in range(out_ref.shape[1] // BLOCK):
                columns = slice(j * BLOCK, (j + 1) * BLOCK)
                kept = stored[:, i : i + 1] if first == 0 else stored[i : i + 1, j : j + 1]
                kept = jnp.broadcast_to(kept.astype(jnp.float32), (BLOCK, BLOCK))
                out_ref[rows, columns] = out_ref[rows, columns] * kept.astype(out_ref.dtype)


def masked(prolong, a_matrix, p_pattern, a_pattern):
    return pl.pallas_call(
        mask_kernel,
        out_shape=[jax.ShapeDtypeStruct(v.shape, v.dtype) for v in (prolong, a_matrix)],
        in_specs=[ANY] * 4,
        out_specs=[VMEM, VMEM],
        scratch_shapes=[
            pltpu.VMEM(p_pattern.shape[::-1], p_pattern.dtype),
            pltpu.VMEM(a_pattern.shape, a_pattern.dtype),
            pltpu.SemaphoreType.DMA((4,)),
        ],
        compiler_params=pltpu.CompilerParams(vmem_limit_bytes=61 << 20),
        cost_estimate=pl.CostEstimate(flops=a_matrix.size, bytes_accessed=4 << 20, transcendentals=0),
    )(prolong, a_matrix, p_pattern.T, a_pattern)


def pair_kernel(one, two, out_ref):
    out_ref[0] = one[...]
    out_ref[1] = two[...]


def paired(one, two):
    cost = pl.CostEstimate(flops=0, bytes_accessed=8 * one.size, transcendentals=0)
    return on_device(pair_kernel, (2, *one.shape), one.dtype, [VMEM] * 2, cost=cost)(one, two)


def line_up_kernel(spot_ref, own, above, below, up_two, down_two, p_ref):
    z, y, xh = spot_ref[0], spot_ref[1], spot_ref[2]
    blocks = [own.at[0], above.at[0], down_two, below.at[1], own.at[1], above.at[1], up_two, below.at[0]]
    for d, block in enumerate(blocks):
        place_in = lax.rem(z + d - 2 * y - 1 + 2 * PLANES, PLANES)
        odd = (place_in < LANES).astype(jnp.int32)
        shift = jnp.where(odd == 1, place_in, PLANES - 1 - place_in)
        side = lax.rem(odd + xh, 2)
        column = pl.multiple_of(lax.rem(y + shift, LANES) * BLOCK, BLOCK)
        p_ref[side, :, pl.ds(column, BLOCK)] = block[...]


def line_up(spot, *blocks):
    size = blocks[0].shape[1]
    return on_device(
        line_up_kernel, (2, size, LANES * BLOCK), jnp.bfloat16, [SMEM] + [VMEM] * len(blocks),
        cost=pl.CostEstimate(flops=0, bytes_accessed=4 << 20, transcendentals=0),
    )(spot, *blocks)


def w_kernel(base, p_ref, one, two, *rest):
    out_ref = rest[-1]
    if base:
        out_ref[:base] = rest[0][...]
    size = one.shape[0]
    step = size // 3
    for c in range(0, LANES, 2):
        columns = slice(c * BLOCK, (c + 2) * BLOCK)
        for start in range(0, size, step):
            rows = slice(start, start + step)
            total = dot32(one[rows], p_ref[0, :, columns]) + dot32(two[rows], p_ref[1, :, columns])
            total = total.astype(jnp.bfloat16)
            out_ref[base + c, rows] = total[:, :BLOCK]
            out_ref[base + c + 1, rows] = total[:, BLOCK:]


def w_products(p_all, one, two, *before):
    size = one.shape[0]
    return on_device(
        functools.partial(w_kernel, LANES * len(before)),
        (LANES * (1 + len(before)), size, BLOCK),
        jnp.bfloat16,
        [VMEM] * (3 + len(before)),
        cost=pl.CostEstimate(flops=4 * size * size * LANES * BLOCK, bytes_accessed=6 << 20, transcendentals=0),
        grant=2,
    )(p_all, one, two, *before)


def coarse_chunks(w_ref, pairs, out_ref):
    units = []
    for pair in pairs:
        units += [pair.at[0], pair.at[1]] if len(pair.shape) == 3 else [pair]
    top = jnp.zeros((BLOCK, BLOCK), jnp.float32)
    for i, unit in enumerate(units):
        both = dot32(w_ref[...], unit[...])
        part = both[:BLOCK] + both[BLOCK:]
        out_ref[i, :BLOCK] = part
        top = jnp.maximum(top, jnp.abs(part))
    top = jnp.max(jnp.max(top, axis=0, keepdims=True), axis=1, keepdims=True)
    power = jnp.ceil(jnp.log2(jnp.maximum(top, 1e-30))) - 14.0
    scale = jnp.exp2(-power)
    for i in range(len(units)):
        out_ref[i, :BLOCK] = out_ref[i, :BLOCK] * scale
        out_ref[i, BLOCK:] = jnp.broadcast_to(power, (8, BLOCK))


def own_kernel(parts_ref, *refs):
    pairs, (out_ref, w_ref) = refs[:-2], refs[-2:]
    for start in range(0, parts_ref.shape[1], BLOCK):
        rows = slice(start, start + BLOCK)
        w = parts_ref[0, rows].astype(jnp.float32)
        for i in range(1, parts_ref.shape[0]):
            w += parts_ref[i, rows].astype(jnp.float32)
        turned = w.T
        high = turned.astype(jnp.bfloat16)
        w_ref[:BLOCK, rows] = high
        w_ref[BLOCK:, rows] = (turned - high.astype(jnp.float32)).astype(jnp.bfloat16)
    coarse_chunks(w_ref, pairs, out_ref)


def other_kernel(w_ref, *refs):
    coarse_chunks(w_ref, refs[:-1], refs[-1])


def c_products(parts, pairs, passed):
    size = parts.shape[1]
    cost = pl.CostEstimate(flops=8 * LANES * size * BLOCK * BLOCK, bytes_accessed=4 << 20, transcendentals=0)
    chunks = jax.ShapeDtypeStruct((2 * LANES, BLOCK + 8, BLOCK), jnp.float32)
    own, w_both = pl.pallas_call(
        own_kernel,
        out_shape=[chunks, jax.ShapeDtypeStruct((2 * BLOCK, size), jnp.bfloat16)],
        in_specs=[VMEM] * (len(pairs) + 1),
        out_specs=[VMEM] * 2,
        compiler_params=pltpu.CompilerParams(vmem_limit_bytes=2 << 20),
        cost_estimate=cost,
    )(parts, *pairs)
    other = on_device(
        other_kernel, chunks.shape, chunks.dtype, [VMEM] * (len(passed) + 1), cost=cost, grant=2
    )(w_both, *passed)
    return jnp.concatenate([own, other])


def unpack(parts):
    parts = parts.astype(jnp.float32)
    return jnp.sum(parts[:, :BLOCK] * jnp.exp2(parts[:, BLOCK : BLOCK + 1, :1]), axis=0).T


def both(*values):
    return lax.optimization_barrier(values)


def local(a_matrix, prolong, a_pattern, p_pattern):
    row, col = lax.axis_index("row"), lax.axis_index("col")
    spot = jnp.stack([row // 2, col // 4, (col // 2) % 2]).astype(jnp.int32)
    p_eff, a_eff = masked(prolong, a_matrix, p_pattern, a_pattern)
    first, second = send(p_eff, turn), send(p_eff, turn_far)
    across = send(p_eff, far_x)
    near, distant = send(a_eff, swap), send(a_eff, swap_far)
    pair = paired(p_eff, across)
    first, second, spot = both(first, second, spot)
    own = paired(first, second)
    below, above, pair_1 = both(send(own, z_up), send(own, z_down), send(pair, y_up))
    pair_3 = send(pair, y_down)
    up_two, down_two = send(below[0], z_up), send(above[0], z_down)
    up_two, down_two, near, distant, pair_3, pair_1 = both(up_two, down_two, near, distant, pair_3, pair_1)
    beyond = send(pair_1[0], y_up), send(pair_3[1], y_down)
    p_all = line_up(spot, own, above, below, up_two, down_two)
    near_2, distant_2 = send(near, other_core), send(distant, other_core)
    w_part = w_products(p_all, near, distant)
    w_part = w_products(p_all, near_2, distant_2, w_part)
    w_part, pair, pair_1, pair_3, *beyond = both(w_part, pair, pair_1, pair_3, *beyond)
    pairs = [pair, pair_1, *beyond, pair_3]
    passed = [send(p, other_core) for p in pairs]
    w_parts = lax.all_to_all(w_part, AXES, 0, 0, axis_index_groups=W_GROUPS, tiled=True)
    c_part = c_products(w_parts, pairs, passed).astype(jnp.float16)
    return unpack(lax.all_to_all(c_part, AXES, 0, 0, axis_index_groups=C_GROUPS, tiled=True))


def solution(mesh):
    placed = (P("row", "col"),) * 4
    return jax.shard_map(
        local, mesh=mesh, in_specs=placed, out_specs=P("row", "col"), check_vma=False
    )
```

```python
import functools

import jax
import jax.numpy as jnp
from jax import lax
from jax.experimental import pallas as pl
from jax.experimental.pallas import tpu as pltpu
from jax.sharding import PartitionSpec as P

BLOCK = 128
AXES = ("row", "col")
PLANES, LANES = 8, 4


def place(z, xl, y, xh, k):
    return (2 * (z % PLANES) + xl) * 16 + 4 * (y % LANES) + 2 * xh + k


SPOTS = [
    (z, xl, y, xh, k)
    for z in range(PLANES)
    for xl in range(2)
    for y in range(LANES)
    for xh in range(2)
    for k in range(2)
]


def send(value, target):
    pairs = [(place(*spot), place(*target(*spot))) for spot in SPOTS]
    return lax.ppermute(value, AXES, pairs)


def turn(z, xl, y, xh, k):
    shift = (y - z // 2) % LANES
    return (z + shift if z % 2 else z - shift), xl, z // 2, xh, k


def turn_far(z, xl, y, xh, k):
    z_to, *rest = turn(z, xl, y, xh, k)
    return z_to + PLANES // 2, *rest


def z_up(z, xl, y, xh, k):
    return z + 1, xl, y, xh, k


def z_down(z, xl, y, xh, k):
    return z - 1, xl, y, xh, k


def y_up(z, xl, y, xh, k):
    return z, xl, y + 1, xh, k


def y_down(z, xl, y, xh, k):
    return z, xl, y - 1, xh, k


def far_x(z, xl, y, xh, k):
    return z, xl, y, 1 - xh, k


def other_core(z, xl, y, xh, k):
    return z, xl, y, xh, 1 - k


def swap(z, xl, y, xh, k):
    return z, k, y, xh, xl


def swap_far(z, xl, y, xh, k):
    return z, k, y, 1 - xh, xl


W_GROUPS = [
    [place(z, s ^ k, y, xh, k) for s in range(2) for y in range(LANES)]
    for z in range(PLANES)
    for xh in range(2)
    for k in range(2)
]


def coarse_row(y, xh, k, dk, dy, dx):
    i = 4 * ((y - dy) % LANES) + 2 * (xh ^ dx) + (k ^ dk)
    return i // 2, i % 2


C_GROUPS = [
    [
        place(*coarse_row(y, xh, k, dk, dy, dx), y, xh, k)
        for dk in range(2)
        for dy in range(LANES)
        for dx in range(2)
    ]
    for y in range(LANES)
    for xh in range(2)
    for k in range(2)
]


VMEM = pl.BlockSpec(memory_space=pltpu.VMEM)
SMEM = pl.BlockSpec(memory_space=pltpu.SMEM)
ANY = pl.BlockSpec(memory_space=pl.ANY)


def on_device(kernel, shape, dtype, specs, scratch=(), cost=None, grant=0.25):
    return pl.pallas_call(
        kernel,
        out_shape=jax.ShapeDtypeStruct(shape, dtype),
        in_specs=specs,
        out_specs=VMEM,
        scratch_shapes=scratch,
        compiler_params=pltpu.CompilerParams(vmem_limit_bytes=int(grant * 2**20)),
        cost_estimate=cost,
    )


def dot32(a, b):
    return jnp.dot(a, b, preferred_element_type=jnp.float32)


def mask_kernel(p_any, a_any, p_pattern, a_pattern, p_out, a_out, p_stored, a_stored, sems):
    moves = [(p_pattern, p_stored), (p_any, p_out), (a_pattern, a_stored), (a_any, a_out)]
    copies = [pltpu.make_async_copy(*move, sems.at[i]) for i, move in enumerate(moves)]
    for copy in copies:
        copy.start()
    for first, stored, out_ref in ((0, p_stored, p_out), (2, a_stored, a_out)):
        copies[first].wait()
        copies[first + 1].wait()
        for i in range(out_ref.shape[0] // BLOCK):
            rows = slice(i * BLOCK, (i + 1) * BLOCK)
            for j in range(out_ref.shape[1] // BLOCK):
                columns = slice(j * BLOCK, (j + 1) * BLOCK)
                kept = stored[:, i : i + 1] if first == 0 else stored[i : i + 1, j : j + 1]
                kept = jnp.broadcast_to(kept.astype(jnp.float32), (BLOCK, BLOCK))
                out_ref[rows, columns] = out_ref[rows, columns] * kept.astype(out_ref.dtype)


def masked(prolong, a_matrix, p_pattern, a_pattern):
    return pl.pallas_call(
        mask_kernel,
        out_shape=[jax.ShapeDtypeStruct(v.shape, v.dtype) for v in (prolong, a_matrix)],
        in_specs=[ANY] * 4,
        out_specs=[VMEM, VMEM],
        scratch_shapes=[
            pltpu.VMEM(p_pattern.shape[::-1], p_pattern.dtype),
            pltpu.VMEM(a_pattern.shape, a_pattern.dtype),
            pltpu.SemaphoreType.DMA((4,)),
        ],
        compiler_params=pltpu.CompilerParams(vmem_limit_bytes=61 << 20),
        cost_estimate=pl.CostEstimate(flops=a_matrix.size, bytes_accessed=4 << 20, transcendentals=0),
    )(prolong, a_matrix, p_pattern.T, a_pattern)


def pair_kernel(one, two, out_ref):
    out_ref[0] = one[...]
    out_ref[1] = two[...]


def paired(one, two):
    cost = pl.CostEstimate(flops=0, bytes_accessed=8 * one.size, transcendentals=0)
    return on_device(pair_kernel, (2, *one.shape), one.dtype, [VMEM] * 2, cost=cost)(one, two)


def line_up_kernel(spot_ref, own, above, below, up_two, down_two, p_ref):
    z, y, xh = spot_ref[0], spot_ref[1], spot_ref[2]
    blocks = [own.at[0], above.at[0], down_two, below.at[1], own.at[1], above.at[1], up_two, below.at[0]]
    for d, block in enumerate(blocks):
        place_in = lax.rem(z + d - 2 * y - 1 + 2 * PLANES, PLANES)
        odd = (place_in < LANES).astype(jnp.int32)
        shift = jnp.where(odd == 1, place_in, PLANES - 1 - place_in)
        side = lax.rem(odd + xh, 2)
        column = pl.multiple_of(lax.rem(y + shift, LANES) * BLOCK, BLOCK)
        p_ref[side, :, pl.ds(column, BLOCK)] = block[...]


def line_up(spot, *blocks):
    size = blocks[0].shape[1]
    return on_device(
        line_up_kernel, (2, size, LANES * BLOCK), jnp.bfloat16, [SMEM] + [VMEM] * len(blocks),
        cost=pl.CostEstimate(flops=0, bytes_accessed=4 << 20, transcendentals=0),
    )(spot, *blocks)


def w_kernel(base, p_ref, one, two, *rest):
    out_ref = rest[-1]
    if base:
        out_ref[:base] = rest[0][...]
    size = one.shape[0]
    step = size // 3
    for c in range(0, LANES, 2):
        columns = slice(c * BLOCK, (c + 2) * BLOCK)
        for start in range(0, size, step):
            rows = slice(start, start + step)
            total = dot32(one[rows], p_ref[0, :, columns]) + dot32(two[rows], p_ref[1, :, columns])
            total = total.astype(jnp.bfloat16)
            out_ref[base + c, rows] = total[:, :BLOCK]
            out_ref[base + c + 1, rows] = total[:, BLOCK:]


def w_products(p_all, one, two, *before):
    size = one.shape[0]
    return on_device(
        functools.partial(w_kernel, LANES * len(before)),
        (LANES * (1 + len(before)), size, BLOCK),
        jnp.bfloat16,
        [VMEM] * (3 + len(before)),
        cost=pl.CostEstimate(flops=4 * size * size * LANES * BLOCK, bytes_accessed=6 << 20, transcendentals=0),
        grant=2,
    )(p_all, one, two, *before)


def coarse_chunks(w_ref, pairs, out_ref):
    units = []
    for pair in pairs:
        units += [pair.at[0], pair.at[1]] if len(pair.shape) == 3 else [pair]
    top = jnp.zeros((BLOCK, BLOCK), jnp.float32)
    for i, unit in enumerate(units):
        both = dot32(w_ref[...], unit[...])
        part = both[:BLOCK] + both[BLOCK:]
        out_ref[i, :BLOCK] = part
        top = jnp.maximum(top, jnp.abs(part))
    top = jnp.max(jnp.max(top, axis=0, keepdims=True), axis=1, keepdims=True)
    power = jnp.ceil(jnp.log2(jnp.maximum(top, 1e-30))) - 14.0
    scale = jnp.exp2(-power)
    for i in range(len(units)):
        out_ref[i, :BLOCK] = out_ref[i, :BLOCK] * scale
        out_ref[i, BLOCK:] = jnp.broadcast_to(power, (8, BLOCK))


def own_kernel(parts_ref, *refs):
    pairs, (out_ref, w_ref) = refs[:-2], refs[-2:]
    for start in range(0, parts_ref.shape[1], BLOCK):
        rows = slice(start, start + BLOCK)
        w = parts_ref[0, rows].astype(jnp.float32)
        for i in range(1, parts_ref.shape[0]):
            w += parts_ref[i, rows].astype(jnp.float32)
        turned = w.T
        high = turned.astype(jnp.bfloat16)
        w_ref[:BLOCK, rows] = high
        w_ref[BLOCK:, rows] = (turned - high.astype(jnp.float32)).astype(jnp.bfloat16)
    coarse_chunks(w_ref, pairs, out_ref)


def other_kernel(w_ref, *refs):
    coarse_chunks(w_ref, refs[:-1], refs[-1])


def c_products(parts, pairs, passed):
    size = parts.shape[1]
    cost = pl.CostEstimate(flops=8 * LANES * size * BLOCK * BLOCK, bytes_accessed=4 << 20, transcendentals=0)
    chunks = jax.ShapeDtypeStruct((2 * LANES, BLOCK + 8, BLOCK), jnp.float32)
    own, w_both = pl.pallas_call(
        own_kernel,
        out_shape=[chunks, jax.ShapeDtypeStruct((2 * BLOCK, size), jnp.bfloat16)],
        in_specs=[VMEM] * (len(pairs) + 1),
        out_specs=[VMEM] * 2,
        compiler_params=pltpu.CompilerParams(vmem_limit_bytes=2 << 20),
        cost_estimate=cost,
    )(parts, *pairs)
    other = on_device(
        other_kernel, chunks.shape, chunks.dtype, [VMEM] * (len(passed) + 1), cost=cost, grant=2
    )(w_both, *passed)
    return jnp.concatenate([own, other])


def unpack(parts):
    parts = parts.astype(jnp.float32)
    return jnp.sum(parts[:, :BLOCK] * jnp.exp2(parts[:, BLOCK : BLOCK + 1, :1]), axis=0).T


def both(*values):
    return lax.optimization_barrier(values)


def local(a_matrix, prolong, a_pattern, p_pattern):
    row, col = lax.axis_index("row"), lax.axis_index("col")
    spot = jnp.stack([row // 2, col // 4, (col // 2) % 2]).astype(jnp.int32)
    p_eff, a_eff = masked(prolong, a_matrix, p_pattern, a_pattern)
    first, second = send(p_eff, turn), send(p_eff, turn_far)
    across = send(p_eff, far_x)
    distant, near = send(a_eff, swap_far), send(a_eff, swap)
    pair = paired(p_eff, across)
    first, second, spot = both(first, second, spot)
    own = paired(first, second)
    below, above, pair_1 = both(send(own, z_up), send(own, z_down), send(pair, y_up))
    pair_3 = send(pair, y_down)
    up_two, down_two = send(below[0], z_up), send(above[0], z_down)
    up_two, down_two, distant, near, pair_3, pair_1 = both(up_two, down_two, distant, near, pair_3, pair_1)
    beyond = send(pair_1[0], y_up), send(pair_3[1], y_down)
    p_all = line_up(spot, own, above, below, up_two, down_two)
    distant_2, near_2 = send(distant, other_core), send(near, other_core)
    w_part = w_products(p_all, near, distant)
    w_part = w_products(p_all, near_2, distant_2, w_part)
    w_part, pair, pair_1, pair_3, *beyond = both(w_part, pair, pair_1, pair_3, *beyond)
    pairs = [pair, pair_1, *beyond, pair_3]
    passed = [send(p, other_core) for p in pairs]
    w_parts = lax.all_to_all(w_part, AXES, 0, 0, axis_index_groups=W_GROUPS, tiled=True)
    c_part = c_products(w_parts, pairs, passed).astype(jnp.float16)
    return unpack(lax.all_to_all(c_part, AXES, 0, 0, axis_index_groups=C_GROUPS, tiled=True))


def solution(mesh):
    placed = (P("row", "col"),) * 4
    return jax.shard_map(
        local, mesh=mesh, in_specs=placed, out_specs=P("row", "col"), check_vma=False
    )
```

```python
import functools

import jax
import jax.numpy as jnp
from jax import lax
from jax.experimental import pallas as pl
from jax.experimental.pallas import tpu as pltpu
from jax.sharding import PartitionSpec as P

BLOCK = 128
AXES = ("row", "col")
PLANES, LANES = 8, 4


def place(z, xl, y, xh, k):
    return (2 * (z % PLANES) + xl) * 16 + 4 * (y % LANES) + 2 * xh + k


SPOTS = [
    (z, xl, y, xh, k)
    for z in range(PLANES)
    for xl in range(2)
    for y in range(LANES)
    for xh in range(2)
    for k in range(2)
]


def send(value, target):
    pairs = [(place(*spot), place(*target(*spot))) for spot in SPOTS]
    return lax.ppermute(value, AXES, pairs)


def turn(z, xl, y, xh, k):
    shift = (y - z // 2) % LANES
    return (z + shift if z % 2 else z - shift), xl, z // 2, xh, k


def turn_far(z, xl, y, xh, k):
    z_to, *rest = turn(z, xl, y, xh, k)
    return z_to + PLANES // 2, *rest


def z_up(z, xl, y, xh, k):
    return z + 1, xl, y, xh, k


def z_down(z, xl, y, xh, k):
    return z - 1, xl, y, xh, k


def y_up(z, xl, y, xh, k):
    return z, xl, y + 1, xh, k


def y_down(z, xl, y, xh, k):
    return z, xl, y - 1, xh, k


def far_x(z, xl, y, xh, k):
    return z, xl, y, 1 - xh, k


def other_core(z, xl, y, xh, k):
    return z, xl, y, xh, 1 - k


def swap(z, xl, y, xh, k):
    return z, k, y, xh, xl


def swap_far(z, xl, y, xh, k):
    return z, k, y, 1 - xh, xl


W_GROUPS = [
    [place(z, s ^ k, y, xh, k) for s in range(2) for y in range(LANES)]
    for z in range(PLANES)
    for xh in range(2)
    for k in range(2)
]


def coarse_row(y, xh, k, dk, dy, dx):
    i = 4 * ((y - dy) % LANES) + 2 * (xh ^ dx) + (k ^ dk)
    return i // 2, i % 2


C_GROUPS = [
    [
        place(*coarse_row(y, xh, k, dk, dy, dx), y, xh, k)
        for dk in range(2)
        for dy in range(LANES)
        for dx in range(2)
    ]
    for y in range(LANES)
    for xh in range(2)
    for k in range(2)
]


VMEM = pl.BlockSpec(memory_space=pltpu.VMEM)
SMEM = pl.BlockSpec(memory_space=pltpu.SMEM)
ANY = pl.BlockSpec(memory_space=pl.ANY)


def on_device(kernel, shape, dtype, specs, scratch=(), cost=None, grant=0.25):
    return pl.pallas_call(
        kernel,
        out_shape=jax.ShapeDtypeStruct(shape, dtype),
        in_specs=specs,
        out_specs=VMEM,
        scratch_shapes=scratch,
        compiler_params=pltpu.CompilerParams(vmem_limit_bytes=int(grant * 2**20)),
        cost_estimate=cost,
    )


def dot32(a, b):
    return jnp.dot(a, b, preferred_element_type=jnp.float32)


def mask_kernel(p_any, a_any, p_pattern, a_pattern, p_out, a_out, p_stored, a_stored, sems):
    moves = [(p_pattern, p_stored), (p_any, p_out), (a_pattern, a_stored), (a_any, a_out)]
    copies = [pltpu.make_async_copy(*move, sems.at[i]) for i, move in enumerate(moves)]
    for copy in copies:
        copy.start()
    for first, stored, out_ref in ((0, p_stored, p_out), (2, a_stored, a_out)):
        copies[first].wait()
        copies[first + 1].wait()
        for i in range(out_ref.shape[0] // BLOCK):
            rows = slice(i * BLOCK, (i + 1) * BLOCK)
            for j in range(out_ref.shape[1] // BLOCK):
                columns = slice(j * BLOCK, (j + 1) * BLOCK)
                kept = stored[:, i : i + 1] if first == 0 else stored[i : i + 1, j : j + 1]
                kept = jnp.broadcast_to(kept.astype(jnp.float32), (BLOCK, BLOCK))
                out_ref[rows, columns] = out_ref[rows, columns] * kept.astype(out_ref.dtype)


def masked(prolong, a_matrix, p_pattern, a_pattern):
    return pl.pallas_call(
        mask_kernel,
        out_shape=[jax.ShapeDtypeStruct(v.shape, v.dtype) for v in (prolong, a_matrix)],
        in_specs=[ANY] * 4,
        out_specs=[VMEM, VMEM],
        scratch_shapes=[
            pltpu.VMEM(p_pattern.shape[::-1], p_pattern.dtype),
            pltpu.VMEM(a_pattern.shape, a_pattern.dtype),
            pltpu.SemaphoreType.DMA((4,)),
        ],
        compiler_params=pltpu.CompilerParams(vmem_limit_bytes=61 << 20),
        cost_estimate=pl.CostEstimate(flops=a_matrix.size, bytes_accessed=4 << 20, transcendentals=0),
    )(prolong, a_matrix, p_pattern.T, a_pattern)


def pair_kernel(one, two, out_ref):
    out_ref[0] = one[...]
    out_ref[1] = two[...]


def paired(one, two):
    cost = pl.CostEstimate(flops=0, bytes_accessed=8 * one.size, transcendentals=0)
    return on_device(pair_kernel, (2, *one.shape), one.dtype, [VMEM] * 2, cost=cost)(one, two)


def line_up_kernel(spot_ref, own, above, below, up_two, down_two, p_ref):
    z, y, xh = spot_ref[0], spot_ref[1], spot_ref[2]
    blocks = [own.at[0], above.at[0], down_two, below.at[1], own.at[1], above.at[1], up_two, below.at[0]]
    for d, block in enumerate(blocks):
        place_in = lax.rem(z + d - 2 * y - 1 + 2 * PLANES, PLANES)
        odd = (place_in < LANES).astype(jnp.int32)
        shift = jnp.where(odd == 1, place_in, PLANES - 1 - place_in)
        side = lax.rem(odd + xh, 2)
        column = pl.multiple_of(lax.rem(y + shift, LANES) * BLOCK, BLOCK)
        p_ref[side, :, pl.ds(column, BLOCK)] = block[...]


def line_up(spot, *blocks):
    size = blocks[0].shape[1]
    return on_device(
        line_up_kernel, (2, size, LANES * BLOCK), jnp.bfloat16, [SMEM] + [VMEM] * len(blocks),
        cost=pl.CostEstimate(flops=0, bytes_accessed=4 << 20, transcendentals=0),
    )(spot, *blocks)


def w_kernel(base, p_ref, one, two, *rest):
    out_ref = rest[-1]
    if base:
        out_ref[:base] = rest[0][...]
    size = one.shape[0]
    step = size // 3
    for c in range(0, LANES, 2):
        columns = slice(c * BLOCK, (c + 2) * BLOCK)
        for start in range(0, size, step):
            rows = slice(start, start + step)
            total = dot32(one[rows], p_ref[0, :, columns]) + dot32(two[rows], p_ref[1, :, columns])
            total = total.astype(jnp.bfloat16)
            out_ref[base + c, rows] = total[:, :BLOCK]
            out_ref[base + c + 1, rows] = total[:, BLOCK:]


def w_products(p_all, one, two, *before):
    size = one.shape[0]
    return on_device(
        functools.partial(w_kernel, LANES * len(before)),
        (LANES * (1 + len(before)), size, BLOCK),
        jnp.bfloat16,
        [VMEM] * (3 + len(before)),
        cost=pl.CostEstimate(flops=4 * size * size * LANES * BLOCK, bytes_accessed=6 << 20, transcendentals=0),
        grant=2,
    )(p_all, one, two, *before)


def coarse_chunks(w_ref, pairs, out_ref):
    units = []
    for pair in pairs:
        units += [pair.at[0], pair.at[1]] if len(pair.shape) == 3 else [pair]
    top = jnp.zeros((BLOCK, BLOCK), jnp.float32)
    for i, unit in enumerate(units):
        both = dot32(w_ref[...], unit[...])
        part = both[:BLOCK] + both[BLOCK:]
        out_ref[i, :BLOCK] = part
        top = jnp.maximum(top, jnp.abs(part))
    top = jnp.max(jnp.max(top, axis=0, keepdims=True), axis=1, keepdims=True)
    power = jnp.ceil(jnp.log2(jnp.maximum(top, 1e-30))) - 14.0
    scale = jnp.exp2(-power)
    for i in range(len(units)):
        out_ref[i, :BLOCK] = out_ref[i, :BLOCK] * scale
        out_ref[i, BLOCK:] = jnp.broadcast_to(power, (8, BLOCK))


def own_kernel(parts_ref, *refs):
    pairs, (out_ref, w_ref) = refs[:-2], refs[-2:]
    for start in range(0, parts_ref.shape[1], BLOCK):
        rows = slice(start, start + BLOCK)
        w = parts_ref[0, rows].astype(jnp.float32)
        for i in range(1, parts_ref.shape[0]):
            w += parts_ref[i, rows].astype(jnp.float32)
        turned = w.T
        high = turned.astype(jnp.bfloat16)
        w_ref[:BLOCK, rows] = high
        w_ref[BLOCK:, rows] = (turned - high.astype(jnp.float32)).astype(jnp.bfloat16)
    coarse_chunks(w_ref, pairs, out_ref)


def other_kernel(w_ref, *refs):
    coarse_chunks(w_ref, refs[:-1], refs[-1])


def c_products(parts, pairs, passed):
    size = parts.shape[1]
    cost = pl.CostEstimate(flops=8 * LANES * size * BLOCK * BLOCK, bytes_accessed=4 << 20, transcendentals=0)
    chunks = jax.ShapeDtypeStruct((2 * LANES, BLOCK + 8, BLOCK), jnp.float32)
    own, w_both = pl.pallas_call(
        own_kernel,
        out_shape=[chunks, jax.ShapeDtypeStruct((2 * BLOCK, size), jnp.bfloat16)],
        in_specs=[VMEM] * (len(pairs) + 1),
        out_specs=[VMEM] * 2,
        compiler_params=pltpu.CompilerParams(vmem_limit_bytes=2 << 20),
        cost_estimate=cost,
    )(parts, *pairs)
    other = on_device(
        other_kernel, chunks.shape, chunks.dtype, [VMEM] * (len(passed) + 1), cost=cost, grant=2
    )(w_both, *passed)
    return jnp.concatenate([own, other])


def unpack(parts):
    parts = parts.astype(jnp.float32)
    return jnp.sum(parts[:, :BLOCK] * jnp.exp2(parts[:, BLOCK : BLOCK + 1, :1]), axis=0).T


def both(*values):
    return lax.optimization_barrier(values)


def local(a_matrix, prolong, a_pattern, p_pattern):
    row, col = lax.axis_index("row"), lax.axis_index("col")
    spot = jnp.stack([row // 2, col // 4, (col // 2) % 2]).astype(jnp.int32)
    p_eff, a_eff = masked(prolong, a_matrix, p_pattern, a_pattern)
    second, first = send(p_eff, turn_far), send(p_eff, turn)
    across = send(p_eff, far_x)
    distant, near = send(a_eff, swap_far), send(a_eff, swap)
    pair = paired(p_eff, across)
    second, first, spot = both(second, first, spot)
    own = paired(first, second)
    below, above, pair_1 = both(send(own, z_up), send(own, z_down), send(pair, y_up))
    pair_3 = send(pair, y_down)
    up_two, down_two = send(below[0], z_up), send(above[0], z_down)
    up_two, down_two, distant, near, pair_3, pair_1 = both(up_two, down_two, distant, near, pair_3, pair_1)
    beyond = send(pair_1[0], y_up), send(pair_3[1], y_down)
    p_all = line_up(spot, own, above, below, up_two, down_two)
    distant_2, near_2 = send(distant, other_core), send(near, other_core)
    w_part = w_products(p_all, near, distant)
    w_part = w_products(p_all, near_2, distant_2, w_part)
    w_part, pair, pair_1, pair_3, *beyond = both(w_part, pair, pair_1, pair_3, *beyond)
    pairs = [pair, pair_1, *beyond, pair_3]
    passed = [send(p, other_core) for p in pairs]
    w_parts = lax.all_to_all(w_part, AXES, 0, 0, axis_index_groups=W_GROUPS, tiled=True)
    c_part = c_products(w_parts, pairs, passed).astype(jnp.float16)
    return unpack(lax.all_to_all(c_part, AXES, 0, 0, axis_index_groups=C_GROUPS, tiled=True))


def solution(mesh):
    placed = (P("row", "col"),) * 4
    return jax.shard_map(
        local, mesh=mesh, in_specs=placed, out_specs=P("row", "col"), check_vma=False
    )
```

```python
import functools

import jax
import jax.numpy as jnp
from jax import lax
from jax.experimental import pallas as pl
from jax.experimental.pallas import tpu as pltpu
from jax.sharding import PartitionSpec as P

BLOCK = 128
AXES = ("row", "col")
PLANES, LANES = 8, 4


def place(z, xl, y, xh, k):
    return (2 * (z % PLANES) + xl) * 16 + 4 * (y % LANES) + 2 * xh + k


SPOTS = [
    (z, xl, y, xh, k)
    for z in range(PLANES)
    for xl in range(2)
    for y in range(LANES)
    for xh in range(2)
    for k in range(2)
]


def send(value, target):
    pairs = [(place(*spot), place(*target(*spot))) for spot in SPOTS]
    return lax.ppermute(value, AXES, pairs)


def turn(z, xl, y, xh, k):
    shift = (y - z // 2) % LANES
    return (z + shift if z % 2 else z - shift), xl, z // 2, xh, k


def turn_far(z, xl, y, xh, k):
    z_to, *rest = turn(z, xl, y, xh, k)
    return z_to + PLANES // 2, *rest


def z_up(z, xl, y, xh, k):
    return z + 1, xl, y, xh, k


def z_down(z, xl, y, xh, k):
    return z - 1, xl, y, xh, k


def y_up(z, xl, y, xh, k):
    return z, xl, y + 1, xh, k


def y_down(z, xl, y, xh, k):
    return z, xl, y - 1, xh, k


def far_x(z, xl, y, xh, k):
    return z, xl, y, 1 - xh, k


def other_core(z, xl, y, xh, k):
    return z, xl, y, xh, 1 - k


def swap(z, xl, y, xh, k):
    return z, k, y, xh, xl


def swap_far(z, xl, y, xh, k):
    return z, k, y, 1 - xh, xl


W_GROUPS = [
    [place(z, s ^ k, y, xh, k) for s in range(2) for y in range(LANES)]
    for z in range(PLANES)
    for xh in range(2)
    for k in range(2)
]


def coarse_row(y, xh, k, dk, dy, dx):
    i = 4 * ((y - dy) % LANES) + 2 * (xh ^ dx) + (k ^ dk)
    return i // 2, i % 2


C_GROUPS = [
    [
        place(*coarse_row(y, xh, k, dk, dy, dx), y, xh, k)
        for dk in range(2)
        for dy in range(LANES)
        for dx in range(2)
    ]
    for y in range(LANES)
    for xh in range(2)
    for k in range(2)
]


VMEM = pl.BlockSpec(memory_space=pltpu.VMEM)
SMEM = pl.BlockSpec(memory_space=pltpu.SMEM)
ANY = pl.BlockSpec(memory_space=pl.ANY)


def on_device(kernel, shape, dtype, specs, scratch=(), cost=None, grant=0.25):
    return pl.pallas_call(
        kernel,
        out_shape=jax.ShapeDtypeStruct(shape, dtype),
        in_specs=specs,
        out_specs=VMEM,
        scratch_shapes=scratch,
        compiler_params=pltpu.CompilerParams(vmem_limit_bytes=int(grant * 2**20)),
        cost_estimate=cost,
    )


def dot32(a, b):
    return jnp.dot(a, b, preferred_element_type=jnp.float32)


def mask_kernel(p_any, a_any, p_pattern, a_pattern, p_out, a_out, p_stored, a_stored, sems):
    moves = [(p_pattern, p_stored), (p_any, p_out), (a_pattern, a_stored), (a_any, a_out)]
    copies = [pltpu.make_async_copy(*move, sems.at[i]) for i, move in enumerate(moves)]
    for copy in reversed(copies):
        copy.start()
    for first, stored, out_ref in ((0, p_stored, p_out), (2, a_stored, a_out)):
        copies[first].wait()
        copies[first + 1].wait()
        for i in range(out_ref.shape[0] // BLOCK):
            rows = slice(i * BLOCK, (i + 1) * BLOCK)
            for j in range(out_ref.shape[1] // BLOCK):
                columns = slice(j * BLOCK, (j + 1) * BLOCK)
                kept = stored[:, i : i + 1] if first == 0 else stored[i : i + 1, j : j + 1]
                kept = jnp.broadcast_to(kept.astype(jnp.float32), (BLOCK, BLOCK))
                out_ref[rows, columns] = out_ref[rows, columns] * kept.astype(out_ref.dtype)


def masked(prolong, a_matrix, p_pattern, a_pattern):
    return pl.pallas_call(
        mask_kernel,
        out_shape=[jax.ShapeDtypeStruct(v.shape, v.dtype) for v in (prolong, a_matrix)],
        in_specs=[ANY] * 4,
        out_specs=[VMEM, VMEM],
        scratch_shapes=[
            pltpu.VMEM(p_pattern.shape[::-1], p_pattern.dtype),
            pltpu.VMEM(a_pattern.shape, a_pattern.dtype),
            pltpu.SemaphoreType.DMA((4,)),
        ],
        compiler_params=pltpu.CompilerParams(vmem_limit_bytes=61 << 20),
        cost_estimate=pl.CostEstimate(flops=a_matrix.size, bytes_accessed=4 << 20, transcendentals=0),
    )(prolong, a_matrix, p_pattern.T, a_pattern)


def pair_kernel(one, two, out_ref):
    out_ref[0] = one[...]
    out_ref[1] = two[...]


def paired(one, two):
    cost = pl.CostEstimate(flops=0, bytes_accessed=8 * one.size, transcendentals=0)
    return on_device(pair_kernel, (2, *one.shape), one.dtype, [VMEM] * 2, cost=cost)(one, two)


def line_up_kernel(spot_ref, own, above, below, up_two, down_two, p_ref):
    z, y, xh = spot_ref[0], spot_ref[1], spot_ref[2]
    blocks = [own.at[0], above.at[0], down_two, below.at[1], own.at[1], above.at[1], up_two, below.at[0]]
    for d, block in enumerate(blocks):
        place_in = lax.rem(z + d - 2 * y - 1 + 2 * PLANES, PLANES)
        odd = (place_in < LANES).astype(jnp.int32)
        shift = jnp.where(odd == 1, place_in, PLANES - 1 - place_in)
        side = lax.rem(odd + xh, 2)
        column = pl.multiple_of(lax.rem(y + shift, LANES) * BLOCK, BLOCK)
        p_ref[side, :, pl.ds(column, BLOCK)] = block[...]


def line_up(spot, *blocks):
    size = blocks[0].shape[1]
    return on_device(
        line_up_kernel, (2, size, LANES * BLOCK), jnp.bfloat16, [SMEM] + [VMEM] * len(blocks),
        cost=pl.CostEstimate(flops=0, bytes_accessed=4 << 20, transcendentals=0),
    )(spot, *blocks)


def w_kernel(base, p_ref, one, two, *rest):
    out_ref = rest[-1]
    if base:
        out_ref[:base] = rest[0][...]
    size = one.shape[0]
    step = size // 3
    for c in range(0, LANES, 2):
        columns = slice(c * BLOCK, (c + 2) * BLOCK)
        for start in range(0, size, step):
            rows = slice(start, start + step)
            total = dot32(one[rows], p_ref[0, :, columns]) + dot32(two[rows], p_ref[1, :, columns])
            total = total.astype(jnp.bfloat16)
            out_ref[base + c, rows] = total[:, :BLOCK]
            out_ref[base + c + 1, rows] = total[:, BLOCK:]


def w_products(p_all, one, two, *before):
    size = one.shape[0]
    return on_device(
        functools.partial(w_kernel, LANES * len(before)),
        (LANES * (1 + len(before)), size, BLOCK),
        jnp.bfloat16,
        [VMEM] * (3 + len(before)),
        cost=pl.CostEstimate(flops=4 * size * size * LANES * BLOCK, bytes_accessed=6 << 20, transcendentals=0),
        grant=2,
    )(p_all, one, two, *before)


def coarse_chunks(w_ref, pairs, out_ref):
    units = []
    for pair in pairs:
        units += [pair.at[0], pair.at[1]] if len(pair.shape) == 3 else [pair]
    top = jnp.zeros((BLOCK, BLOCK), jnp.float32)
    for i, unit in enumerate(units):
        both = dot32(w_ref[...], unit[...])
        part = both[:BLOCK] + both[BLOCK:]
        out_ref[i, :BLOCK] = part
        top = jnp.maximum(top, jnp.abs(part))
    top = jnp.max(jnp.max(top, axis=0, keepdims=True), axis=1, keepdims=True)
    power = jnp.ceil(jnp.log2(jnp.maximum(top, 1e-30))) - 14.0
    scale = jnp.exp2(-power)
    for i in range(len(units)):
        out_ref[i, :BLOCK] = out_ref[i, :BLOCK] * scale
        out_ref[i, BLOCK:] = jnp.broadcast_to(power, (8, BLOCK))


def own_kernel(parts_ref, *refs):
    pairs, (out_ref, w_ref) = refs[:-2], refs[-2:]
    for start in range(0, parts_ref.shape[1], BLOCK):
        rows = slice(start, start + BLOCK)
        w = parts_ref[0, rows].astype(jnp.float32)
        for i in range(1, parts_ref.shape[0]):
            w += parts_ref[i, rows].astype(jnp.float32)
        turned = w.T
        high = turned.astype(jnp.bfloat16)
        w_ref[:BLOCK, rows] = high
        w_ref[BLOCK:, rows] = (turned - high.astype(jnp.float32)).astype(jnp.bfloat16)
    coarse_chunks(w_ref, pairs, out_ref)


def other_kernel(w_ref, *refs):
    coarse_chunks(w_ref, refs[:-1], refs[-1])


def c_products(parts, pairs, passed):
    size = parts.shape[1]
    cost = pl.CostEstimate(flops=8 * LANES * size * BLOCK * BLOCK, bytes_accessed=4 << 20, transcendentals=0)
    chunks = jax.ShapeDtypeStruct((2 * LANES, BLOCK + 8, BLOCK), jnp.float32)
    own, w_both = pl.pallas_call(
        own_kernel,
        out_shape=[chunks, jax.ShapeDtypeStruct((2 * BLOCK, size), jnp.bfloat16)],
        in_specs=[VMEM] * (len(pairs) + 1),
        out_specs=[VMEM] * 2,
        compiler_params=pltpu.CompilerParams(vmem_limit_bytes=2 << 20),
        cost_estimate=cost,
    )(parts, *pairs)
    other = on_device(
        other_kernel, chunks.shape, chunks.dtype, [VMEM] * (len(passed) + 1), cost=cost, grant=2
    )(w_both, *passed)
    return jnp.concatenate([own, other])


def unpack(parts):
    parts = parts.astype(jnp.float32)
    return jnp.sum(parts[:, :BLOCK] * jnp.exp2(parts[:, BLOCK : BLOCK + 1, :1]), axis=0).T


def both(*values):
    return lax.optimization_barrier(values)


def local(a_matrix, prolong, a_pattern, p_pattern):
    row, col = lax.axis_index("row"), lax.axis_index("col")
    spot = jnp.stack([row // 2, col // 4, (col // 2) % 2]).astype(jnp.int32)
    p_eff, a_eff = masked(prolong, a_matrix, p_pattern, a_pattern)
    first, second = send(p_eff, turn), send(p_eff, turn_far)
    across = send(p_eff, far_x)
    distant, near = send(a_eff, swap_far), send(a_eff, swap)
    pair = paired(p_eff, across)
    first, second, spot = both(first, second, spot)
    own = paired(first, second)
    below, above, pair_1 = both(send(own, z_up), send(own, z_down), send(pair, y_up))
    pair_3 = send(pair, y_down)
    up_two, down_two = send(below[0], z_up), send(above[0], z_down)
    up_two, down_two, distant, near, pair_3, pair_1 = both(up_two, down_two, distant, near, pair_3, pair_1)
    beyond = send(pair_1[0], y_up), send(pair_3[1], y_down)
    p_all = line_up(spot, own, above, below, up_two, down_two)
    distant_2, near_2 = send(distant, other_core), send(near, other_core)
    w_part = w_products(p_all, near, distant)
    w_part = w_products(p_all, near_2, distant_2, w_part)
    w_part, pair, pair_1, pair_3, *beyond = both(w_part, pair, pair_1, pair_3, *beyond)
    pairs = [pair, pair_1, *beyond, pair_3]
    passed = [send(p, other_core) for p in pairs]
    w_parts = lax.all_to_all(w_part, AXES, 0, 0, axis_index_groups=W_GROUPS, tiled=True)
    c_part = c_products(w_parts, pairs, passed).astype(jnp.float16)
    return unpack(lax.all_to_all(c_part, AXES, 0, 0, axis_index_groups=C_GROUPS, tiled=True))


def solution(mesh):
    placed = (P("row", "col"),) * 4
    return jax.shard_map(
        local, mesh=mesh, in_specs=placed, out_specs=P("row", "col"), check_vma=False
    )
```
